512 devices in a mesh: img: 8 (over x, core), sp: 64 (over y, z).
Axes of the slice: x: 4, y: 8, z: 8, core: 2. Of those that a mesh axis runs over, the one named last changes fastest.
Arguments:
- tokens: bfloat16 [8, 64, 16, 16, 768], P('img', 'sp'), may hold values from -6 to 6
- w_qkv: bfloat16 [768, 1152], P('img'), may hold values from -0.21875 to 0.21875
- score_scale: float32 [6], replicated, may hold values from 5 to 20
- grad_out: bfloat16 [8, 64, 16, 16, 384], P('img', 'sp'), may hold values from -1.75 to 1.75
Outputs:
- attended: bfloat16 [8, 64, 16, 16, 384], P('img', 'sp')
- grad_tokens: bfloat16 [8, 64, 16, 16, 768], P('img', 'sp')
- weight_grad: float32 [768, 1152], P('img', 'sp')
The draws below stay inside these ranges and needn't reach their ends.
All inputs are finite; a program needn't handle non-finite values.
Results may differ from the reference program's by a relative error of at most 0.018.
Values may be sent and summed in bfloat16 or wider, within the bound.
A program may use at most 64 MiB of HBM per device.

```python
import math
import jax
import jax.numpy as jnp
from jax import lax

D = 768
HEAD_DIM = 64
HEADS_WIN = 6
GRID = 128
COLS = 128
RADIUS = 3
IMGS = 8
TILE_R = 16
TILE_C = 16
WIN_WIDTH = 384
N_SP = 64


def with_spikes(array, rng, source, target, parts, factor):
    owner, partner = [(jnp.arange(array.shape[position]) // (array.shape[position] // parts)).reshape([-1 if axis == position else 1 for axis in range(array.ndim)]) for position in (source, target)]
    chosen = jax.random.permutation(rng, parts)[partner]
    strong = (owner == chosen) | (owner == (partner + parts // 2) % parts)
    return jnp.where(strong, factor * array, array)


def block_scale(rng, extent, split, least, top_value):
    def one(axis_at, parts):
        heights = jax.random.uniform(jax.random.fold_in(jax.random.fold_in(rng, 6), axis_at), (parts,), jnp.float32, least / len(split), top_value / len(split))
        return jnp.repeat(jnp.exp(heights), extent[axis_at] // parts).reshape((-1,) + (1,) * (len(extent) - axis_at - 1))

    loudness = one(*split[0])
    for cut in split[1:]:
        loudness = loudness * one(*cut)
    return loudness


def normal_values(key, shape, scale, limit, cuts=(), held_as=jnp.bfloat16):
    entries = jax.random.normal(key, shape, jnp.float32) * scale
    if len(cuts) > 0:
        entries = block_scale(key, shape, cuts, -0.22, 0.18) * entries
    return jnp.clip(entries, min=-limit, max=limit).astype(held_as)


def heavy_noise(own_key, shape, spread, limit, shards, heavy, kind=jnp.bfloat16):
    drawn = spread * jax.random.normal(own_key, shape, jnp.float32)
    if shards:
        drawn = drawn * block_scale(own_key, shape, shards, -0.22, 0.18)
    return jnp.clip(with_spikes(drawn, jax.random.fold_in(own_key, 3), *heavy), -limit, limit).astype(kind)


def setup_inputs(seed: int = 0) -> dict:
    arg_keys = jax.random.split(jax.random.key(seed), 5)
    tokens = normal_values(arg_keys[0], (IMGS, N_SP, TILE_R, TILE_C, D), 1.0, 6.0, ((0, 8), (1, 64)))
    w_qkv = normal_values(arg_keys[1], (D, 3 * WIN_WIDTH), D ** -0.5, 0.21875, ((0, 8),))
    score_scale = jnp.clip(jnp.exp(jax.random.uniform(arg_keys[2], (HEADS_WIN,), jnp.float32, math.log(5.0), math.log(20.0))), 5.0, 20.0)
    grad_out = heavy_noise(arg_keys[3], (IMGS, N_SP, TILE_R, TILE_C, WIN_WIDTH), 0.1, 1.75, ((0, 8), (1, 64)), (1, 4, 64, 4.0))
    return dict(tokens=tokens, w_qkv=w_qkv, score_scale=score_scale, grad_out=grad_out)


norm_eps = 1e-06

def block_pass(query_block, kv_block, grad_block, row_first, col_first, scales, radius, grid_rows, grid_cols):
    local_rows, local_cols, width = query_block.shape
    heads = scales.shape[0]
    head_size = width // heads
    ext_rows = kv_block.shape[0]
    ext_cols = kv_block.shape[1]
    query_flat = query_block.reshape(local_rows * local_cols, width).astype(jnp.float32)
    kv_flat = kv_block.reshape(ext_rows * ext_cols, 2 * width)
    key_flat = kv_flat[:, :width].astype(jnp.float32)
    value_flat = kv_flat[:, width:]
    grad_flat = grad_block.reshape(local_rows * local_cols, width)
    query_pos = jnp.arange(local_rows * local_cols, dtype=jnp.int32)
    key_pos = jnp.arange(ext_rows * ext_cols, dtype=jnp.int32)
    query_row = (query_pos // local_cols)[:, None]
    query_col = (query_pos % local_cols)[:, None]
    key_row = (key_pos // ext_cols)[None, :]
    key_col = (key_pos % ext_cols)[None, :]
    global_row = row_first.astype(jnp.int32) + key_row - radius
    global_col = col_first.astype(jnp.int32) + key_col - radius
    allowed = (jnp.abs(key_row - radius - query_row) <= radius) & (jnp.abs(key_col - radius - query_col) <= radius)
    allowed = allowed & (global_row >= 0) & (global_row < grid_rows) & (global_col >= 0) & (global_col < grid_cols)
    scale_root = 1.0 / math.sqrt(head_size)
    outputs, query_grads, key_grads, value_grads = ([], [], [], [])
    for head_index in range(heads):
        lower = head_index * head_size
        upper = lower + head_size
        query_head = query_flat[:, lower:upper]
        key_head = key_flat[:, lower:upper]
        value_head = value_flat[:, lower:upper]
        grad_head = grad_flat[:, lower:upper]
        query_inv = lax.rsqrt(lax.optimization_barrier(jnp.mean(query_head * query_head, axis=-1, keepdims=True)) + norm_eps) * scale_root
        key_inv = lax.rsqrt(lax.optimization_barrier(jnp.mean(key_head * key_head, axis=-1, keepdims=True)) + norm_eps) * scale_root
        query_unit = (query_head * query_inv).astype(jnp.bfloat16)
        key_unit = (key_head * key_inv).astype(jnp.bfloat16)
        scores = scales[head_index] * lax.dot_general(query_unit, key_unit, (((1,), (1,)), ((), ())), preferred_element_type=jnp.float32)
        raised = jnp.where(allowed, jnp.exp(scores), jnp.zeros_like(scores))
        attention = raised / lax.optimization_barrier(jnp.sum(raised, axis=-1, keepdims=True))
        attention_low = attention.astype(jnp.bfloat16)
        outputs.append(jnp.dot(attention_low, value_head, preferred_element_type=jnp.float32))
        value_grads.append(lax.dot_general(attention_low, grad_head, (((0,), (0,)), ((), ())), preferred_element_type=jnp.float32))
        grad_attention = lax.dot_general(grad_head, value_head, (((1,), (1,)), ((), ())), preferred_element_type=jnp.float32)
        row_total = lax.optimization_barrier(jnp.sum(attention * grad_attention, axis=-1, keepdims=True))
        grad_scores = (scales[head_index] * attention * (grad_attention - row_total)).astype(jnp.bfloat16)
        grad_qunit = jnp.dot(grad_scores, key_unit, preferred_element_type=jnp.float32)
        grad_kunit = lax.dot_general(grad_scores, query_unit, (((0,), (0,)), ((), ())), preferred_element_type=jnp.float32)
        query_grads.append(query_inv * (grad_qunit - query_head * (query_inv * query_inv * head_size) * lax.optimization_barrier(jnp.mean(grad_qunit * query_head, axis=-1, keepdims=True))))
        key_grads.append(key_inv * (grad_kunit - key_head * (key_inv * key_inv * head_size) * lax.optimization_barrier(jnp.mean(grad_kunit * key_head, axis=-1, keepdims=True))))
    attended = jnp.concatenate(outputs, axis=-1).astype(jnp.bfloat16).reshape(local_rows, local_cols, width)
    query_grad = jnp.concatenate(query_grads, axis=-1).reshape(local_rows, local_cols, width)
    kv_grad = jnp.concatenate(key_grads + value_grads, axis=-1).reshape(ext_rows, ext_cols, 2 * width)
    return (attended, query_grad, kv_grad)

def untile(tiled):
    row_tiles = GRID // TILE_R
    col_tiles = COLS // TILE_C
    last = tiled.shape[-1]
    return tiled.reshape(row_tiles, col_tiles, TILE_R, TILE_C, last).transpose(0, 2, 1, 3, 4).reshape(GRID, COLS, last)

def retile(full):
    row_tiles = GRID // TILE_R
    col_tiles = COLS // TILE_C
    last = full.shape[-1]
    return full.reshape(row_tiles, TILE_R, col_tiles, TILE_C, last).transpose(0, 2, 1, 3, 4).reshape(row_tiles * col_tiles, TILE_R, TILE_C, last)

def reference(tokens, w_qkv, score_scale, grad_out):
    width = HEADS_WIN * HEAD_DIM
    col_tiles = COLS // TILE_C
    tile_count = GRID // TILE_R * col_tiles
    ext_rows = TILE_R + 2 * RADIUS
    ext_cols = TILE_C + 2 * RADIUS

    def one_image(running, pair):
        image, grad_image = pair
        flat = image.reshape(tile_count * TILE_R * TILE_C, D)
        qkv_tiles = jnp.dot(flat, w_qkv, preferred_element_type=jnp.float32).astype(jnp.bfloat16).reshape(tile_count, TILE_R, TILE_C, 3 * width)
        queries = qkv_tiles[..., :width]
        padded = jnp.pad(untile(qkv_tiles[..., width:]), ((RADIUS, RADIUS), (RADIUS, RADIUS), (0, 0)))

        def one_block(tile_index):
            row_first = (tile_index // col_tiles * TILE_R).astype(jnp.int32)
            col_first = (tile_index % col_tiles * TILE_C).astype(jnp.int32)
            kv_block = lax.dynamic_slice(padded, (row_first, col_first, jnp.int32(0)), (ext_rows, ext_cols, 2 * width))
            return block_pass(queries[tile_index], kv_block, grad_image[tile_index], row_first, col_first, score_scale, RADIUS, GRID, COLS)
        attended, query_grad, kv_grad = lax.map(one_block, jnp.arange(tile_count, dtype=jnp.int32))

        def add_block(tile_index, kv_total):
            row_first = (tile_index // col_tiles * TILE_R).astype(jnp.int32)
            col_first = (tile_index % col_tiles * TILE_C).astype(jnp.int32)
            start = (row_first, col_first, jnp.int32(0))
            current = lax.dynamic_slice(kv_total, start, (ext_rows, ext_cols, 2 * width))
            return lax.dynamic_update_slice(kv_total, current + kv_grad[tile_index], start)
        kv_total = lax.fori_loop(0, tile_count, add_block, jnp.zeros((GRID + 2 * RADIUS, COLS + 2 * RADIUS, 2 * width), jnp.float32))
        kv_tiles = retile(kv_total[RADIUS:RADIUS + GRID, RADIUS:RADIUS + COLS])
        grad_qkv = jnp.concatenate([query_grad, kv_tiles], axis=-1).astype(jnp.bfloat16).reshape(tile_count * TILE_R * TILE_C, 3 * width)
        grad_image_tokens = lax.dot_general(grad_qkv, w_qkv, (((1,), (1,)), ((), ())), preferred_element_type=jnp.float32).astype(jnp.bfloat16).reshape(tile_count, TILE_R, TILE_C, D)
        running = running + lax.dot_general(flat, grad_qkv, (((0,), (0,)), ((), ())), preferred_element_type=jnp.float32)
        return (running, (attended, grad_image_tokens))
    total, (attended, grad_tokens) = lax.scan(one_image, jnp.zeros((D, 3 * width), jnp.float32), (tokens, grad_out))
    return (attended, grad_tokens, total / IMGS)
```

```python
import math

import jax
import jax.numpy as jnp
from jax import lax
from jax.experimental import pallas as pl
from jax.experimental.pallas import tpu as pltpu
from jax.sharding import PartitionSpec as P

MESH = pl.DeviceIdType.MESH
BF16 = jnp.bfloat16
F32 = jnp.float32
GRID = 128
COLS = 128
RADIUS = 3


norm_eps = 1e-06


def passed_along(x, axis, by):
    peers = lax.axis_size(axis)
    pairs = [(i, i + by) for i in range(peers) if 0 <= i + by < peers]
    return lax.ppermute(x, axis, pairs)


def block_pass(
    query_block, kv_block, grad_block, row_first, col_first, scales, radius, grid_rows, grid_cols
):
    local_rows, local_cols, width = query_block.shape
    heads = scales.shape[0]
    head_size = width // heads
    ext_rows = kv_block.shape[0]
    ext_cols = kv_block.shape[1]
    query_flat = query_block.reshape(local_rows * local_cols, width).astype(jnp.float32)
    kv_flat = kv_block.reshape(ext_rows * ext_cols, 2 * width)
    key_flat = kv_flat[:, :width].astype(jnp.float32)
    value_flat = kv_flat[:, width:]
    grad_flat = grad_block.reshape(local_rows * local_cols, width)
    query_pos = jnp.arange(local_rows * local_cols, dtype=jnp.int32)
    key_pos = jnp.arange(ext_rows * ext_cols, dtype=jnp.int32)
    query_row = (query_pos // local_cols)[:, None]
    query_col = (query_pos % local_cols)[:, None]
    key_row = (key_pos // ext_cols)[None, :]
    key_col = (key_pos % ext_cols)[None, :]
    global_row = row_first + key_row - radius
    global_col = col_first + key_col - radius
    allowed = (jnp.abs(key_row - radius - query_row) <= radius) & (
        jnp.abs(key_col - radius - query_col) <= radius
    )
    allowed = (
        allowed
        & (global_row >= 0)
        & (global_row < grid_rows)
        & (global_col >= 0)
        & (global_col < grid_cols)
    )
    scale_root = 1.0 / math.sqrt(head_size)
    outputs, query_grads, key_grads, value_grads = ([], [], [], [])
    for head_index in range(heads):
        lower = head_index * head_size
        upper = lower + head_size
        query_head = query_flat[:, lower:upper]
        key_head = key_flat[:, lower:upper]
        value_head = value_flat[:, lower:upper]
        grad_head = grad_flat[:, lower:upper]
        query_inv = (
            lax.rsqrt(jnp.mean(query_head * query_head, axis=-1, keepdims=True) + norm_eps)
            * scale_root
        )
        key_inv = (
            lax.rsqrt(jnp.mean(key_head * key_head, axis=-1, keepdims=True) + norm_eps) * scale_root
        )
        query_unit = (query_head * query_inv).astype(jnp.bfloat16)
        key_unit = (key_head * key_inv).astype(jnp.bfloat16)
        scores = scales[head_index] * lax.dot_general(
            query_unit, key_unit, (((1,), (1,)), ((), ())), preferred_element_type=jnp.float32
        )
        raised = jnp.where(allowed, jnp.exp(scores), jnp.zeros_like(scores))
        attention = raised / jnp.sum(raised, axis=-1, keepdims=True)
        attention_low = attention.astype(jnp.bfloat16)
        outputs.append(jnp.dot(attention_low, value_head, preferred_element_type=jnp.float32))
        value_grads.append(
            lax.dot_general(
                attention_low,
                grad_head,
                (((0,), (0,)), ((), ())),
                preferred_element_type=jnp.float32,
            )
        )
        grad_attention = lax.dot_general(
            grad_head, value_head, (((1,), (1,)), ((), ())), preferred_element_type=jnp.float32
        )
        row_total = jnp.sum(attention * grad_attention, axis=-1, keepdims=True)
        grad_scores = (scales[head_index] * attention * (grad_attention - row_total)).astype(
            jnp.bfloat16
        )
        grad_qunit = jnp.dot(grad_scores, key_unit, preferred_element_type=jnp.float32)
        grad_kunit = lax.dot_general(
            grad_scores, query_unit, (((0,), (0,)), ((), ())), preferred_element_type=jnp.float32
        )
        query_grads.append(
            query_inv
            * (
                grad_qunit
                - query_head
                * (query_inv * query_inv * head_size)
                * jnp.mean(grad_qunit * query_head, axis=-1, keepdims=True)
            )
        )
        key_grads.append(
            key_inv
            * (
                grad_kunit
                - key_head
                * (key_inv * key_inv * head_size)
                * jnp.mean(grad_kunit * key_head, axis=-1, keepdims=True)
            )
        )
    attended = (
        jnp.concatenate(outputs, axis=-1)
        .astype(jnp.bfloat16)
        .reshape(local_rows, local_cols, width)
    )
    query_grad = jnp.concatenate(query_grads, axis=-1).reshape(local_rows, local_cols, width)
    kv_grad = jnp.concatenate(key_grads + value_grads, axis=-1).reshape(
        ext_rows, ext_cols, 2 * width
    )
    return (attended, query_grad, kv_grad)


def own_span(step, size, reach):
    if step < 0:
        return (size - reach, size)
    if step > 0:
        return (0, reach)
    return (0, size)


def ext_span(step, size, reach):
    if step < 0:
        return (0, reach)
    if step > 0:
        return (reach + size, 2 * reach + size)
    return (reach, reach + size)

def remote(src, dst, send, recv, device):
    return pltpu.make_async_remote_copy(
        src_ref=src,
        dst_ref=dst,
        send_sem=send,
        recv_sem=recv,
        device_id=device,
        device_id_type=MESH,
    )


def reduce_kernel(
    tok_ref, gq_ref, out_ref,
    tok_t, s1, r1, s2, r2, acc, acc_t, s3, r3, acc4, s4, r4, fin,
    core_send, core_recv, x_send, x_recv, y_send, y_recv, z_send, z_recv,
):
    img = lax.axis_index("img")
    sp = lax.axis_index("sp")
    x, c = img // 2, img % 2
    y, z = sp // 8, sp % 8
    other_core = (2 * x + 1 - c, sp)
    x_peer = [((2 * ((x + d) % 4) + c), sp) for d in range(4)]
    y_peer = [(img, 8 * ((y + d) % 8) + z) for d in range(8)]
    z_peer = [(img, 8 * y + (z + d) % 8) for d in range(8)]

    barrier = pltpu.get_barrier_semaphore()
    peers = [other_core] + x_peer[1:] + y_peer[1:] + z_peer[1:]
    for peer in peers:
        pl.semaphore_signal(barrier, inc=1, device_id=peer, device_id_type=MESH)

    for b in range(8):
        tok_t[b] = tok_ref[:, 96 * b : 96 * b + 96].astype(F32).T.astype(BF16)
    acc[:, 96:128, :] = jnp.zeros((3, 32, 384), F32)
    acc4[...] = jnp.zeros_like(acc4)
    pl.semaphore_wait(barrier, len(peers))

    def product(p, block):
        return jnp.dot(tok_t[block], gq_ref[p], preferred_element_type=F32)

    core_copies = []
    for p in range(3):
        for k in range(4):
            s1[p, k] = product(p, 2 * k + 1 - c).astype(BF16)
        copy = remote(s1.at[p], r1.at[p], core_send.at[p], core_recv.at[p], other_core)
        copy.start()
        core_copies.append(copy)
    x_copies = []
    for p in range(3):
        core_copies[p].wait()
        for d in range(1, 4):
            to = (x + d) % 4
            s2[p, d - 1] = (product(p, 2 * to + c) + r1[p, to].astype(F32)).astype(BF16)
            copy = remote(
                s2.at[p, d - 1], r2.at[p, d - 1], x_send.at[p, d - 1], x_recv.at[p, d - 1], x_peer[d]
            )
            copy.start()
            x_copies.append(copy)
        acc[p, 0:96] = product(p, img) + r1[p, x].astype(F32)
    for p in range(3):
        total = acc[p, 0:96]
        for d in range(3):
            x_copies[3 * p + d].wait()
            total += r2[p, d].astype(F32)
        acc[p, 0:96] = total
        turned = acc[p].T
        for part in range(3):
            low = 384 * part + 128 * p
            acc_t[low : low + 128] = turned[128 * part : 128 * part + 128]
    y_copies = []
    for d in range(1, 8):
        to = (y + d) % 8
        s3[d - 1] = acc_t[pl.ds(pl.multiple_of(144 * to, 16), 144)].astype(BF16)
        copy = remote(s3.at[d - 1], r3.at[d - 1], y_send.at[d - 1], y_recv.at[d - 1], y_peer[d])
        copy.start()
        y_copies.append(copy)
    total = acc_t[pl.ds(pl.multiple_of(144 * y, 16), 144)]
    for d in range(7):
        y_copies[d].wait()
        total += r3[d].astype(F32)
    acc4[0:144] = total
    for g in range(8):
        s4[g] = acc4[18 * g : 18 * g + 24]
    z_copies = []
    for d in range(1, 8):
        copy = remote(
            s4.at[(z + d) % 8], r4.at[d - 1], z_send.at[d - 1], z_recv.at[d - 1], z_peer[d]
        )
        copy.start()
        z_copies.append(copy)
    total = s4[z]
    for d in range(7):
        z_copies[d].wait()
        total += r4[d]
    fin[...] = jnp.zeros_like(fin)
    fin[0:24] = total * (1.0 / 8.0)
    out_ref[...] = fin[...].T[0:96, 0:18]


def reduced_weight_grad(flat_tokens, grad_parts):
    dma = pltpu.SemaphoreType.DMA
    return pl.pallas_call(
        reduce_kernel,
        out_shape=jax.ShapeDtypeStruct((96, 18), F32),
        in_specs=[pl.BlockSpec(memory_space=pltpu.VMEM)] * 2,
        out_specs=pl.BlockSpec(memory_space=pltpu.VMEM),
        scratch_shapes=[
            pltpu.VMEM((8, 96, 256), BF16),
            pltpu.VMEM((3, 4, 96, 384), BF16),
            pltpu.VMEM((3, 4, 96, 384), BF16),
            pltpu.VMEM((3, 3, 96, 384), BF16),
            pltpu.VMEM((3, 3, 96, 384), BF16),
            pltpu.VMEM((3, 128, 384), F32),
            pltpu.VMEM((1152, 128), F32),
            pltpu.VMEM((7, 144, 128), BF16),
            pltpu.VMEM((7, 144, 128), BF16),
            pltpu.VMEM((152, 128), F32),
            pltpu.VMEM((8, 24, 128), F32),
            pltpu.VMEM((7, 24, 128), F32),
            pltpu.VMEM((128, 128), F32),
            dma((3,)), dma((3,)), dma((3, 3)), dma((3, 3)), dma((7,)), dma((7,)), dma((7,)), dma((7,)),
        ],
        compiler_params=pltpu.CompilerParams(
            collective_id=0, has_side_effects=True, vmem_limit_bytes=32 * 1024 * 1024
        ),
    )(flat_tokens, grad_parts)


def local(tokens, w_qkv, score_scale, grad_out):
    images, tile_one, local_rows, local_cols, model_width = tokens.shape
    triple = w_qkv.shape[1]
    width = triple // 3
    token_count = images * local_rows * local_cols
    col_tiles = COLS // local_cols
    flat_tokens = tokens.reshape(token_count, model_width)
    full_weights = lax.all_gather(w_qkv, "img", axis=0, tiled=True)
    projected = jnp.dot(flat_tokens, full_weights, preferred_element_type=jnp.float32)
    qkv = projected.astype(jnp.bfloat16).reshape(images, local_rows, local_cols, triple)
    queries = qkv[..., :width]
    kv_own = qkv[..., width:]
    ext_rows = local_rows + 2 * RADIUS
    ext_cols = local_cols + 2 * RADIUS
    neighbours = [
        (row_step, col_step)
        for row_step in (-1, 0, 1)
        for col_step in (-1, 0, 1)
        if row_step != 0 or col_step != 0
    ]
    extended = jnp.zeros((images, ext_rows, ext_cols, 2 * width), jnp.bfloat16)
    extended = extended.at[:, RADIUS : RADIUS + local_rows, RADIUS : RADIUS + local_cols].set(
        kv_own
    )
    for row_step, col_step in neighbours:
        row_low, row_high = own_span(row_step, local_rows, RADIUS)
        col_low, col_high = own_span(col_step, local_cols, RADIUS)
        slab = kv_own[:, row_low:row_high, col_low:col_high]
        arrived = passed_along(slab, "sp", -(row_step * col_tiles + col_step))
        erow_low, erow_high = ext_span(row_step, local_rows, RADIUS)
        ecol_low, ecol_high = ext_span(col_step, local_cols, RADIUS)
        extended = extended.at[:, erow_low:erow_high, ecol_low:ecol_high].set(arrived)
    tile_index = lax.axis_index("sp")
    row_first = tile_index // col_tiles * local_rows
    col_first = tile_index % col_tiles * local_cols
    attended_list, query_list, kv_list = ([], [], [])
    attended_one, query_one, kv_one = block_pass(
        queries[0],
        extended[0],
        grad_out[0, 0],
        row_first,
        col_first,
        score_scale,
        RADIUS,
        GRID,
        COLS,
    )
    attended_list.append(attended_one)
    query_list.append(query_one)
    kv_list.append(kv_one)
    attended = jnp.stack(attended_list, axis=0)
    query_grad = jnp.stack(query_list, axis=0)
    kv_grad = jnp.stack(kv_list, axis=0)
    owned = kv_grad[:, RADIUS : RADIUS + local_rows, RADIUS : RADIUS + local_cols]
    for row_step, col_step in neighbours:
        erow_low, erow_high = ext_span(row_step, local_rows, RADIUS)
        ecol_low, ecol_high = ext_span(col_step, local_cols, RADIUS)
        returned = kv_grad[:, erow_low:erow_high, ecol_low:ecol_high]
        arrived = passed_along(
            returned.astype(jnp.bfloat16), "sp", row_step * col_tiles + col_step
        ).astype(returned.dtype)
        row_low, row_high = own_span(row_step, local_rows, RADIUS)
        col_low, col_high = own_span(col_step, local_cols, RADIUS)
        owned = owned.at[:, row_low:row_high, col_low:col_high].add(arrived)
    grad_qkv = (
        jnp.concatenate([query_grad, owned], axis=-1)
        .astype(jnp.bfloat16)
        .reshape(token_count, triple)
    )
    grad_flat = lax.dot_general(
        grad_qkv, full_weights, (((1,), (1,)), ((), ())), preferred_element_type=jnp.float32
    )
    grad_tokens = grad_flat.astype(jnp.bfloat16).reshape(
        images, 1, local_rows, local_cols, model_width
    )
    grad_parts = grad_qkv.reshape(token_count, 3, 3, 128).transpose(2, 0, 1, 3).reshape(3, token_count, 384)
    weight_grad = reduced_weight_grad(flat_tokens, grad_parts)
    return (
        attended.reshape(images, 1, local_rows, local_cols, width),
        grad_tokens,
        weight_grad,
    )


def solution(mesh):
    return jax.shard_map(
        local,
        mesh=mesh,
        in_specs=(
            P("img", "sp", None, None, None),
            P("img", None),
            P(),
            P("img", "sp", None, None, None),
        ),
        out_specs=(
            P("img", "sp", None, None, None),
            P("img", "sp", None, None, None),
            P("img", "sp"),
        ),
        check_vma=False,
    )
```

```python
import jax
import jax.numpy as jnp
from jax import lax
from jax.experimental import pallas as pl
from jax.experimental.pallas import tpu as pltpu
from jax.sharding import PartitionSpec as P

MESH = pl.DeviceIdType.MESH
BF16 = jnp.bfloat16
F32 = jnp.float32
NORM_EPS = 1e-06
NEVER = -1e30
STRIPS = (
    (-1, 0, 0, 48),
    (1, 0, 48, 48),
    (0, -1, 96, 48),
    (0, 1, 144, 48),
    (-1, -1, 192, 16),
    (-1, 1, 208, 16),
    (1, -1, 224, 16),
    (1, 1, 240, 16),
)


def remote(src, dst, send, recv, device):
    return pltpu.make_async_remote_copy(
        src_ref=src,
        dst_ref=dst,
        send_sem=send,
        recv_sem=recv,
        device_id=device,
        device_id_type=MESH,
    )


def dot(a, b):
    return jnp.dot(a, b, preferred_element_type=F32)


def dot_nt(a, b):
    return lax.dot_general(a, b, (((1,), (1,)), ((), ())), preferred_element_type=F32)


def halo_place(j):
    strip = (j >= 48).astype(jnp.int32) + (j >= 96).astype(jnp.int32) + (j >= 144).astype(jnp.int32)
    m = j - 48 * strip
    edge = m >> 4
    along = m & 15
    low = jnp.where((strip & 1) == 0, -3, 16)
    step = jnp.where((strip & 1) == 0, -1, 1)
    level = strip < 2
    row_e = jnp.where(level, low + edge, along)
    col_e = jnp.where(level, along, low + edge)
    rstep_e = jnp.where(level, step, 0)
    cstep_e = jnp.where(level, 0, step)
    k = j - 192
    corner = k >> 4
    n = k & 15
    r3 = n >> 2
    c3 = n & 3
    rstep_c = jnp.where((corner & 2) == 0, -1, 1)
    cstep_c = jnp.where((corner & 1) == 0, -1, 1)
    row_c = jnp.where(rstep_c < 0, -3, 16) + r3
    col_c = jnp.where(cstep_c < 0, -3, 16) + c3
    is_edge = j < 192
    row = jnp.where(is_edge, row_e, row_c)
    col = jnp.where(is_edge, col_e, col_c)
    rstep = jnp.where(is_edge, rstep_e, rstep_c)
    cstep = jnp.where(is_edge, cstep_e, cstep_c)
    filled = is_edge | ((r3 < 3) & (c3 < 3))
    return row, col, rstep, cstep, filled


def owner_token(j):
    row, col, rstep, cstep, filled = halo_place(j)
    return jnp.where(filled, (row - 16 * rstep) * 16 + (col - 16 * cstep), -1)


def kernel(
    tok_ref, w_ref, scale_ref, g_ref, att_ref, gtok_ref, out_ref,
    wp, tok_t, bias, pack, unpack, qkv, inv, qum, gm, kvx, hs, own, ghs, ghr, gq,
    s1, r1, s2, r2, acc, acc_t, s3, r3, acc4, s4, r4, fin,
    wx_send, wx_recv, wc_send, wc_recv, h_send, h_recv, gh_send, gh_recv,
    core_send, core_recv, x_send, x_recv, y_send, y_recv, z_send, z_recv,
):
    img = lax.axis_index("img")
    sp = lax.axis_index("sp")
    x, c = img // 2, img % 2
    y, z = sp // 8, sp % 8
    other_core = (2 * x + 1 - c, sp)
    x_peer = [((2 * ((x + d) % 4) + c), sp) for d in range(4)]
    y_peer = [(img, 8 * ((y + d) % 8) + z) for d in range(8)]
    z_peer = [(img, 8 * y + (z + d) % 8) for d in range(8)]

    def tile_at(rstep, cstep):
        return (img, 8 * ((y + rstep + 8) % 8) + (z + cstep + 8) % 8)

    barrier = pltpu.get_barrier_semaphore()
    peers = [other_core] + x_peer[1:] + y_peer[1:] + z_peer[1:]
    peers += [tile_at(r, s) for r in (-1, 1) for s in (-1, 1)]
    for peer in peers:
        pl.semaphore_signal(barrier, inc=1, device_id=peer, device_id_type=MESH)

    def block(b):
        return pl.ds(pl.multiple_of(96 * b, 32), 96)

    for p in range(3):
        for part in range(3):
            low = 384 * part + 128 * p
            wp[p, block(img), 128 * part : 128 * part + 128] = w_ref[:, low : low + 128]
    pl.semaphore_wait(barrier, len(peers))

    wx, wc = {}, {}
    for p in range(3):
        mine = wp.at[p, block(img)]
        wc[p, 0] = remote(mine, mine, wc_send.at[p, 0], wc_recv.at[p, 0], other_core)
        wc[p, 0].start()
        for d in (1, 3, 2):
            wx[p, d] = remote(mine, mine, wx_send.at[p, d - 1], wx_recv.at[p, d - 1], x_peer[d])
            wx[p, d].start()

    def forward_weights(p):
        for d in (1, 3, 2):
            wx[p, d].wait_recv()
            got = wp.at[p, block(2 * ((x + 4 - d) % 4) + c)]
            wc[p, d] = remote(got, got, wc_send.at[p, d], wc_recv.at[p, d], other_core)
            wc[p, d].start()

    for b in range(8):
        tok_t[b] = tok_ref[:, 96 * b : 96 * b + 96].astype(F32).T.astype(BF16)
    query = lax.broadcasted_iota(jnp.int32, (1, 256), 1)
    query_row, query_col = query >> 4, query & 15

    def put_bias(low, key_row, key_col):
        near = (jnp.abs(key_row - query_row) <= 3) & (jnp.abs(key_col - query_col) <= 3)
        bias[low : low + 256] = jnp.where(near, 0.0, NEVER).astype(F32)

    j_rows = lax.broadcasted_iota(jnp.int32, (256, 1), 0)
    put_bias(0, j_rows >> 4, j_rows & 15)
    row, col, _, _, filled = halo_place(j_rows)
    grow, gcol = row + 16 * y, col + 16 * z
    inside = filled & (grow >= 0) & (grow < 128) & (gcol >= 0) & (gcol < 128)
    put_bias(256, jnp.where(inside, row, 1000), col)
    j_cols = lax.broadcasted_iota(jnp.int32, (1, 256), 1)
    wide_rows = lax.broadcasted_iota(jnp.int32, (256, 256), 0)
    wide_cols = lax.broadcasted_iota(jnp.int32, (256, 256), 1)
    pack[...] = jnp.where(owner_token(j_rows) == wide_cols, 1.0, 0.0).astype(BF16)
    unpack[...] = jnp.where(owner_token(j_cols) == wide_rows, 1.0, 0.0).astype(BF16)
    lane_r = lax.broadcasted_iota(jnp.int32, (128, 128), 0)
    lane_c = lax.broadcasted_iota(jnp.int32, (128, 128), 1)
    same_head = jnp.where((lane_r >> 6) == (lane_c >> 6), 1.0, 0.0).astype(BF16)
    eye = jnp.where(lane_r == lane_c, 1.0, 0.0).astype(BF16)
    lane = lax.broadcasted_iota(jnp.int32, (1, 128), 1)
    head_mask = [jnp.where((lane >> 6) == e, 1.0, 0.0).astype(F32) for e in range(2)]
    for p in range(3):
        g_pair = g_ref[:, 128 * p : 128 * p + 128].astype(F32)
        for e in range(2):
            gm[p, e] = (g_pair * head_mask[e]).astype(BF16)

    def head_sum(v):
        high = v.astype(BF16)
        low = (v - high.astype(F32)).astype(BF16)
        return dot(high, same_head) + dot(low, same_head)

    halo, back = {}, {}

    def project(p):
        for d in range(4):
            wc[p, d].wait_recv()
        low = dot(tok_ref[...], wp[p]).astype(BF16)
        qkv[p] = low
        q = low[:, 0:128].astype(F32)
        k = low[:, 128:256].astype(F32)
        inv_q = lax.rsqrt(head_sum(q * q) * (1.0 / 64.0) + NORM_EPS) * 0.125
        inv_k = lax.rsqrt(head_sum(k * k) * (1.0 / 64.0) + NORM_EPS) * 0.125
        inv[p, :, 0:128] = inv_q
        inv[p, :, 128:256] = inv_k
        q_unit = q * inv_q
        for e in range(2):
            qum[p, e] = (q_unit * head_mask[e]).astype(BF16)
        kvx[p, 0:256, 0:128] = (k * inv_k).astype(BF16)
        kvx[p, 0:256, 128:256] = low[:, 256:384]
        hs[p] = dot(pack[...], kvx[p, 0:256]).astype(BF16)
        for s, (rstep, cstep, first, rows) in enumerate(STRIPS):
            halo[p, s] = remote(
                hs.at[p, pl.ds(first, rows)],
                kvx.at[p, pl.ds(256 + first, rows)],
                h_send.at[p, s],
                h_recv.at[p, s],
                tile_at(-rstep, -cstep),
            )
            halo[p, s].start()

    def attend(p):
        for s in range(8):
            halo[p, s].wait_recv()
        key = kvx[p, :, 0:128]
        value = kvx[p, :, 128:256]
        key_t = dot_nt(eye, key).astype(BF16)
        value_t = dot_nt(eye, value).astype(BF16)
        att_t, gq_t = [], []
        grad_k, grad_v = None, None
        for e in range(2):
            scale = scale_ref[2 * p + e]
            rows = slice(64 * e, 64 * e + 64)
            raised = jnp.exp(dot_nt(key, qum[p, e]) * scale + bias[...])
            attention = raised * (1.0 / jnp.sum(raised, axis=0, keepdims=True))
            att_low = attention.astype(BF16)
            grad_att = dot_nt(value, gm[p, e])
            row_total = jnp.sum(attention * grad_att, axis=0, keepdims=True)
            grad_s = (attention * scale * (grad_att - row_total)).astype(BF16)
            att_t.append(dot(value_t[rows], att_low))
            gq_t.append(dot(key_t[rows], grad_s))
            grad_v_e = dot(att_low, gm[p, e])
            grad_k_e = dot(grad_s, qum[p, e])
            grad_v = grad_v_e if grad_v is None else grad_v + grad_v_e
            grad_k = grad_k_e if grad_k is None else grad_k + grad_k_e
        ghs[p, :, 0:128] = grad_k[256:512].astype(BF16)
        ghs[p, :, 128:256] = grad_v[256:512].astype(BF16)
        for s, (rstep, cstep, first, rows) in enumerate(STRIPS):
            span = pl.ds(first, rows)
            back[p, s] = remote(
                ghs.at[p, span], ghr.at[p, span], gh_send.at[p, s], gh_recv.at[p, s], tile_at(rstep, cstep)
            )
            back[p, s].start()
        own[p, :, 0:128] = grad_k[0:256]
        own[p, :, 128:256] = grad_v[0:256]
        att_ref[:, 128 * p : 128 * p + 128] = jnp.concatenate(att_t, axis=0).T.astype(BF16)
        grad_q = jnp.concatenate(gq_t, axis=0).T
        q = qkv[p, :, 0:128].astype(F32)
        inv_q = inv[p, :, 0:128]
        gq[p, :, 0:128] = (inv_q * (grad_q - q * (inv_q * inv_q) * head_sum(grad_q * q))).astype(BF16)

    def product(p, b):
        return dot(tok_t[b], gq[p])

    core, cross = {}, {}

    def finish(p):
        for s in range(8):
            back[p, s].wait_recv()
        grad_kv = own[p] + dot(unpack[...], ghr[p])
        grad_k = grad_kv[:, 0:128]
        k = qkv[p, :, 128:256].astype(F32)
        inv_k = inv[p, :, 128:256]
        gq[p, :, 128:256] = (inv_k * (grad_k - k * (inv_k * inv_k) * head_sum(grad_k * k))).astype(BF16)
        gq[p, :, 256:384] = grad_kv[:, 128:256].astype(BF16)
        for n in range(4):
            s1[p, n] = product(p, 2 * n + 1 - c).astype(BF16)
        core[p] = remote(s1.at[p], r1.at[p], core_send.at[p], core_recv.at[p], other_core)
        core[p].start()

    def cross_send(p):
        core[p].wait_recv()
        for d in (1, 3, 2):
            to = (x + d) % 4
            s2[p, d - 1] = (product(p, 2 * to + c) + r1[p, to].astype(F32)).astype(BF16)
            cross[p, d] = remote(
                s2.at[p, d - 1], r2.at[p, d - 1], x_send.at[p, d - 1], x_recv.at[p, d - 1], x_peer[d]
            )
            cross[p, d].start()
        acc[p, 0:96] = product(p, img) + r1[p, x].astype(F32)

    def cross_sum(p):
        total = acc[p, 0:96]
        for d in (1, 3, 2):
            cross[p, d].wait_recv()
            total += r2[p, d - 1].astype(F32)
        acc[p, 0:96] = total
        turned = acc[p].T
        for part in range(3):
            low = 384 * part + 128 * p
            acc_t[low : low + 128] = turned[128 * part : 128 * part + 128]

    forward_weights(0)
    project(0)
    forward_weights(1)
    project(1)
    forward_weights(2)
    attend(0)
    project(2)
    attend(1)
    finish(0)
    acc[:, 96:128, :] = jnp.zeros((3, 32, 384), F32)
    acc4[...] = jnp.zeros_like(acc4)
    fin[...] = jnp.zeros_like(fin)
    attend(2)
    finish(1)
    cross_send(0)
    finish(2)
    cross_send(1)
    cross_send(2)
    grad_tokens = dot_nt(gq[0], wp[0]) + dot_nt(gq[1], wp[1]) + dot_nt(gq[2], wp[2])
    gtok_ref[...] = grad_tokens.astype(BF16)
    for p in range(3):
        cross_sum(p)

    y_copies = []
    for d in range(1, 8):
        to = (y + d) % 8
        s3[d - 1] = acc_t[pl.ds(pl.multiple_of(144 * to, 16), 144)].astype(BF16)
        copy = remote(s3.at[d - 1], r3.at[d - 1], y_send.at[d - 1], y_recv.at[d - 1], y_peer[d])
        copy.start()
        y_copies.append(copy)
    total = acc_t[pl.ds(pl.multiple_of(144 * y, 16), 144)]
    for d in range(7):
        y_copies[d].wait_recv()
        total += r3[d].astype(F32)
    acc4[0:144] = total
    for n in range(8):
        s4[n] = acc4[18 * n : 18 * n + 24]
    z_copies = []
    for d in range(1, 8):
        copy = remote(
            s4.at[(z + d) % 8], r4.at[d - 1], z_send.at[d - 1], z_recv.at[d - 1], z_peer[d]
        )
        copy.start()
        z_copies.append(copy)
    total = s4[z]
    for d in range(7):
        z_copies[d].wait_recv()
        total += r4[d]
    fin[0:24] = total * (1.0 / 8.0)
    out_ref[...] = fin[...].T[0:96, 0:18]

    started = list(wx.values()) + list(wc.values()) + list(halo.values()) + list(back.values())
    started += list(core.values()) + list(cross.values()) + y_copies + z_copies
    for copy in started:
        copy.wait_send()


def local(tokens, w_qkv, score_scale, grad_out):
    dma = pltpu.SemaphoreType.DMA
    vmem = pl.BlockSpec(memory_space=pltpu.VMEM)
    attended, grad_tokens, weight_grad = pl.pallas_call(
        kernel,
        out_shape=(
            jax.ShapeDtypeStruct((256, 384), BF16),
            jax.ShapeDtypeStruct((256, 768), BF16),
            jax.ShapeDtypeStruct((96, 18), F32),
        ),
        in_specs=[vmem, vmem, pl.BlockSpec(memory_space=pltpu.SMEM), vmem],
        out_specs=(vmem, vmem, vmem),
        scratch_shapes=[
            pltpu.VMEM((3, 768, 384), BF16),
            pltpu.VMEM((8, 96, 256), BF16),
            pltpu.VMEM((512, 256), F32),
            pltpu.VMEM((256, 256), BF16),
            pltpu.VMEM((256, 256), BF16),
            pltpu.VMEM((3, 256, 384), BF16),
            pltpu.VMEM((3, 256, 256), F32),
            pltpu.VMEM((3, 2, 256, 128), BF16),
            pltpu.VMEM((3, 2, 256, 128), BF16),
            pltpu.VMEM((3, 512, 256), BF16),
            pltpu.VMEM((3, 256, 256), BF16),
            pltpu.VMEM((3, 256, 256), F32),
            pltpu.VMEM((3, 256, 256), BF16),
            pltpu.VMEM((3, 256, 256), BF16),
            pltpu.VMEM((3, 256, 384), BF16),
            pltpu.VMEM((3, 4, 96, 384), BF16),
            pltpu.VMEM((3, 4, 96, 384), BF16),
            pltpu.VMEM((3, 3, 96, 384), BF16),
            pltpu.VMEM((3, 3, 96, 384), BF16),
            pltpu.VMEM((3, 128, 384), F32),
            pltpu.VMEM((1152, 128), F32),
            pltpu.VMEM((7, 144, 128), BF16),
            pltpu.VMEM((7, 144, 128), BF16),
            pltpu.VMEM((152, 128), F32),
            pltpu.VMEM((8, 24, 128), F32),
            pltpu.VMEM((7, 24, 128), F32),
            pltpu.VMEM((128, 128), F32),
            dma((3, 3)), dma((3, 3)), dma((3, 4)), dma((3, 4)),
            dma((3, 8)), dma((3, 8)), dma((3, 8)), dma((3, 8)),
            dma((3,)), dma((3,)), dma((3, 3)), dma((3, 3)),
            dma((7,)), dma((7,)), dma((7,)), dma((7,)),
        ],
        compiler_params=pltpu.CompilerParams(
            collective_id=0, has_side_effects=True, vmem_limit_bytes=40 * 1024 * 1024
        ),
    )(tokens.reshape(256, 768), w_qkv, score_scale, grad_out.reshape(256, 384))
    return (
        attended.reshape(1, 1, 16, 16, 384),
        grad_tokens.reshape(1, 1, 16, 16, 768),
        weight_grad,
    )


def solution(mesh):
    return jax.shard_map(
        local,
        mesh=mesh,
        in_specs=(
            P("img", "sp", None, None, None),
            P("img", None),
            P(),
            P("img", "sp", None, None, None),
        ),
        out_specs=(
            P("img", "sp", None, None, None),
            P("img", "sp", None, None, None),
            P("img", "sp"),
        ),
        check_vma=False,
    )
```

```python
import jax
import jax.numpy as jnp
from jax import lax
from jax.experimental import pallas as pl
from jax.experimental.pallas import tpu as pltpu
from jax.sharding import PartitionSpec as P

MESH = pl.DeviceIdType.MESH
BF16 = jnp.bfloat16
F32 = jnp.float32
NORM_EPS = 1e-06
NEVER = -1e30
STRIPS = (
    (-1, 0, 0, 48),
    (1, 0, 48, 48),
    (0, -1, 96, 48),
    (0, 1, 144, 48),
    (-1, -1, 192, 16),
    (-1, 1, 208, 16),
    (1, -1, 224, 16),
    (1, 1, 240, 16),
)


def remote(src, dst, send, recv, device):
    return pltpu.make_async_remote_copy(
        src_ref=src,
        dst_ref=dst,
        send_sem=send,
        recv_sem=recv,
        device_id=device,
        device_id_type=MESH,
    )


def dot(a, b):
    return jnp.dot(a, b, preferred_element_type=F32)


def dot_nt(a, b):
    return lax.dot_general(a, b, (((1,), (1,)), ((), ())), preferred_element_type=F32)


def halo_place(j):
    strip = (j >= 48).astype(jnp.int32) + (j >= 96).astype(jnp.int32) + (j >= 144).astype(jnp.int32)
    m = j - 48 * strip
    edge = m >> 4
    along = m & 15
    low = jnp.where((strip & 1) == 0, -3, 16)
    step = jnp.where((strip & 1) == 0, -1, 1)
    level = strip < 2
    row_e = jnp.where(level, low + edge, along)
    col_e = jnp.where(level, along, low + edge)
    rstep_e = jnp.where(level, step, 0)
    cstep_e = jnp.where(level, 0, step)
    k = j - 192
    corner = k >> 4
    n = k & 15
    r3 = n >> 2
    c3 = n & 3
    rstep_c = jnp.where((corner & 2) == 0, -1, 1)
    cstep_c = jnp.where((corner & 1) == 0, -1, 1)
    row_c = jnp.where(rstep_c < 0, -3, 16) + r3
    col_c = jnp.where(cstep_c < 0, -3, 16) + c3
    is_edge = j < 192
    row = jnp.where(is_edge, row_e, row_c)
    col = jnp.where(is_edge, col_e, col_c)
    rstep = jnp.where(is_edge, rstep_e, rstep_c)
    cstep = jnp.where(is_edge, cstep_e, cstep_c)
    filled = is_edge | ((r3 < 3) & (c3 < 3))
    return row, col, rstep, cstep, filled


def owner_token(j):
    row, col, rstep, cstep, filled = halo_place(j)
    return jnp.where(filled, (row - 16 * rstep) * 16 + (col - 16 * cstep), -1)


def kernel(
    tok_hbm, w_hbm, scale_hbm, g_hbm, att_hbm, gtok_hbm, out_ref,
    tokx, g_ref, scale_ref, att_ref, gtok_ref, wp, tok_t, tok_2, bias, pack, unpack, qk, inv, qum, gm, kvx, hs, own,
    ghs, ghr, gq, s2, r2, acc, acc_t, ya, zb, sya, szb, rya, rzb, ta, tb, sza, rza, ryb, fin,
    in_sem, w_sem, out_sem, wx_send, wx_recv, wc_send, wc_recv, h_send, h_recv, gh_send, gh_recv,
    tok_send, tok_recv, core_send, core_recv, x_send, x_recv, ya_send, ya_recv, zb_send, zb_recv,
    za_send, za_recv, yb_send, yb_recv,
):
    img = lax.axis_index("img")
    sp = lax.axis_index("sp")
    x, c = img // 2, img % 2
    y, z = sp // 8, sp % 8
    other_core = (2 * x + 1 - c, sp)
    x_peer = [((2 * ((x + d) % 4) + c), sp) for d in range(4)]
    y_peer = [(img, 8 * ((y + d) % 8) + z) for d in range(8)]
    z_peer = [(img, 8 * y + (z + d) % 8) for d in range(8)]

    def tile_at(rstep, cstep):
        return (img, 8 * ((y + rstep + 8) % 8) + (z + cstep + 8) % 8)

    barrier = pltpu.get_barrier_semaphore()
    peers = [other_core] + x_peer[1:] + y_peer[1:] + z_peer[1:]
    peers += [tile_at(r, s) for r in (-1, 1) for s in (-1, 1)]
    for peer in peers:
        pl.semaphore_signal(barrier, inc=1, device_id=peer, device_id_type=MESH)

    def block(b):
        return pl.ds(pl.multiple_of(96 * b, 32), 96)

    loads = [
        pltpu.make_async_copy(tok_hbm, tokx.at[pl.ds(0, 256)], in_sem.at[0]),
        pltpu.make_async_copy(g_hbm, g_ref, in_sem.at[1]),
        pltpu.make_async_copy(scale_hbm, scale_ref, in_sem.at[2]),
    ]
    w_loads = [
        pltpu.make_async_copy(
            w_hbm.at[:, pl.ds(384 * part + 128 * p, 128)],
            wp.at[p, block(img), pl.ds(128 * part, 128)],
            w_sem.at[p, part],
        )
        for p in range(3)
        for part in range(3)
    ]
    for load in w_loads + loads:
        load.start()
    query = lax.broadcasted_iota(jnp.int32, (1, 256), 1)
    query_row, query_col = query >> 4, query & 15

    def put_bias(low, key_row, key_col):
        near = (jnp.abs(key_row - query_row) <= 3) & (jnp.abs(key_col - query_col) <= 3)
        bias[low : low + 256] = jnp.where(near, 0.0, NEVER).astype(F32)

    j_rows = lax.broadcasted_iota(jnp.int32, (256, 1), 0)
    put_bias(0, j_rows >> 4, j_rows & 15)
    row, col, _, _, filled = halo_place(j_rows)
    grow, gcol = row + 16 * y, col + 16 * z
    inside = filled & (grow >= 0) & (grow < 128) & (gcol >= 0) & (gcol < 128)
    put_bias(256, jnp.where(inside, row, 1000), col)
    j_cols = lax.broadcasted_iota(jnp.int32, (1, 256), 1)
    wide_rows = lax.broadcasted_iota(jnp.int32, (256, 256), 0)
    wide_cols = lax.broadcasted_iota(jnp.int32, (256, 256), 1)
    pack[...] = jnp.where(owner_token(j_rows) == wide_cols, 1.0, 0.0).astype(BF16)
    unpack[...] = jnp.where(owner_token(j_cols) == wide_rows, 1.0, 0.0).astype(BF16)
    lane_r = lax.broadcasted_iota(jnp.int32, (128, 128), 0)
    lane_c = lax.broadcasted_iota(jnp.int32, (128, 128), 1)
    same_head = jnp.where((lane_r >> 6) == (lane_c >> 6), 1.0, 0.0).astype(BF16)
    eye = jnp.where(lane_r == lane_c, 1.0, 0.0).astype(BF16)
    lane = lax.broadcasted_iota(jnp.int32, (1, 128), 1)
    head_mask = [jnp.where((lane >> 6) == e, 1.0, 0.0).astype(F32) for e in range(2)]

    for load in w_loads:
        load.wait()
    pl.semaphore_wait(barrier, len(peers))

    wx, wc = {}, {}

    def to_core(p, n, ref):
        wc[p, n] = remote(ref, ref, wc_send.at[p, n], wc_recv.at[p, n], other_core)
        wc[p, n].start()

    def to_x(p, n, ref, d):
        wx[p, n] = remote(ref, ref, wx_send.at[p, n], wx_recv.at[p, n], x_peer[d])
        wx[p, n].start()

    def half(b, h):
        return pl.ds(pl.multiple_of(96 * b + 48 * h, 16), 48)

    left, right, across = [2 * ((x + d) % 4) + c for d in (3, 1, 2)]
    for p in range(3):
        mine = wp.at[p, block(img)]
        to_x(p, 0, mine, 1)
        to_x(p, 1, mine, 3)
        to_core(p, 0, mine)

    for load in loads:
        load.wait()
    hs[...] = dot(pack[...], tokx[0:256]).astype(BF16)
    halo = {}
    for s, (rstep, cstep, first, rows) in reversed(list(enumerate(STRIPS))):
        halo[s] = remote(
            hs.at[pl.ds(first, rows)],
            tokx.at[pl.ds(256 + first, rows)],
            h_send.at[s],
            h_recv.at[s],
            tile_at(-rstep, -cstep),
        )
        halo[s].start()

    def pass_on(p):
        wx[p, 0].wait_recv()
        to_x(p, 2, wp.at[p, half(left, 0)], 1)
        to_core(p, 1, wp.at[p, block(left)])
        wx[p, 1].wait_recv()
        to_x(p, 3, wp.at[p, half(right, 1)], 3)
        to_core(p, 2, wp.at[p, block(right)])

    def pass_core(p):
        for h in range(2):
            wx[p, 2 + h].wait_recv()
            to_core(p, 3 + h, wp.at[p, half(across, h)])

    for p in range(3):
        g_pair = g_ref[:, 128 * p : 128 * p + 128].astype(F32)
        for e in range(2):
            gm[p, e] = (g_pair * head_mask[e]).astype(BF16)

    for b in range(8):
        tok_t[b // 2, b % 2] = tokx[0:256, 96 * b : 96 * b + 96].astype(F32).T.astype(BF16)
    tokens_out = remote(
        tok_t.at[:, 1 - c], tok_2.at[:, :, pl.ds(256, 256)], tok_send, tok_recv, other_core
    )
    tokens_out.start()
    tok_2[:, :, 0:256] = tok_t[:, c]

    def head_sum(v):
        high = v.astype(BF16)
        low = (v - high.astype(F32)).astype(BF16)
        return dot(high, same_head) + dot(low, same_head)

    back, core, cross = {}, {}, {}

    def exchange(p, n, lanes):
        core[p, n] = remote(
            gq.at[p, pl.ds(0, 256), lanes],
            gq.at[p, pl.ds(256, 256), lanes],
            core_send.at[p, n],
            core_recv.at[p, n],
            other_core,
        )
        core[p, n].start()

    def project(p):
        for n in range(5):
            wc[p, n].wait_recv()
        low = dot(tokx[0:256], wp[p]).astype(BF16)
        far = dot(tokx[256:512], wp[p, :, 128:384]).astype(BF16)
        qk[p] = low[:, 0:256]
        q = low[:, 0:128].astype(F32)
        k = low[:, 128:256].astype(F32)
        k_far = far[:, 0:128].astype(F32)
        inv_q = lax.rsqrt(head_sum(q * q) * (1.0 / 64.0) + NORM_EPS) * 0.125
        inv_k = lax.rsqrt(head_sum(k * k) * (1.0 / 64.0) + NORM_EPS) * 0.125
        inv_far = lax.rsqrt(head_sum(k_far * k_far) * (1.0 / 64.0) + NORM_EPS) * 0.125
        inv[p, :, 0:128] = inv_q
        inv[p, :, 128:256] = inv_k
        q_unit = q * inv_q
        for e in range(2):
            qum[p, e] = (q_unit * head_mask[e]).astype(BF16)
        kvx[p, 0:256, 0:128] = (k * inv_k).astype(BF16)
        kvx[p, 0:256, 128:256] = low[:, 256:384]
        kvx[p, 256:512, 0:128] = (k_far * inv_far).astype(BF16)
        kvx[p, 256:512, 128:256] = far[:, 128:256]

    def attend(p):
        key = kvx[p, :, 0:128]
        value = kvx[p, :, 128:256]
        key_t = dot_nt(eye, key).astype(BF16)
        value_t = dot_nt(eye, value).astype(BF16)
        att_t, gq_t = [], []
        grad_k, grad_v = None, None
        for e in range(2):
            scale = scale_ref[2 * p + e]
            rows = slice(64 * e, 64 * e + 64)
            raised = jnp.exp(dot_nt(key, qum[p, e]) * scale + bias[...])
            attention = raised * (1.0 / jnp.sum(raised, axis=0, keepdims=True))
            att_low = attention.astype(BF16)
            grad_att = dot_nt(value, gm[p, e])
            row_total = jnp.sum(attention * grad_att, axis=0, keepdims=True)
            grad_s = (attention * scale * (grad_att - row_total)).astype(BF16)
            att_t.append(dot(value_t[rows], att_low))
            gq_t.append(dot(key_t[rows], grad_s))
            grad_v_e = dot(att_low, gm[p, e])
            grad_k_e = dot(grad_s, qum[p, e])
            grad_v = grad_v_e if grad_v is None else grad_v + grad_v_e
            grad_k = grad_k_e if grad_k is None else grad_k + grad_k_e
        ghs[p, :, 0:128] = grad_k[256:512].astype(BF16)
        ghs[p, :, 128:256] = grad_v[256:512].astype(BF16)
        for s, (rstep, cstep, first, rows) in enumerate(STRIPS):
            span = pl.ds(first, rows)
            back[p, s] = remote(
                ghs.at[p, span], ghr.at[p, span], gh_send.at[p, s], gh_recv.at[p, s], tile_at(rstep, cstep)
            )
            back[p, s].start()
        own[p, :, 0:128] = grad_k[0:256]
        own[p, :, 128:256] = grad_v[0:256]
        att_ref[:, 128 * p : 128 * p + 128] = jnp.concatenate(att_t, axis=0).T.astype(BF16)
        grad_q = jnp.concatenate(gq_t, axis=0).T
        q = qk[p, :, 0:128].astype(F32)
        inv_q = inv[p, :, 0:128]
        gq[p, 0:256, 0:128] = (inv_q * (grad_q - q * (inv_q * inv_q) * head_sum(grad_q * q))).astype(BF16)
        exchange(p, 0, pl.ds(0, 128))

    def finish(p):
        for s in range(8):
            back[p, s].wait_recv()
        grad_kv = own[p] + dot(unpack[...], ghr[p])
        grad_k = grad_kv[:, 0:128]
        k = qk[p, :, 128:256].astype(F32)
        inv_k = inv[p, :, 128:256]
        gq[p, 0:256, 128:256] = (inv_k * (grad_k - k * (inv_k * inv_k) * head_sum(grad_k * k))).astype(BF16)
        gq[p, 0:256, 256:384] = grad_kv[:, 128:256].astype(BF16)
        exchange(p, 1, pl.ds(128, 256))

    def cross_send(p, part):
        core[p, part].wait_recv()
        lanes = slice(128, 384) if part else slice(0, 128)
        span = pl.ds(128, 256) if part else pl.ds(0, 128)
        mine = gq[p, :, lanes]
        for d in (2, 1, 3):
            s2[p, d - 1, :, lanes] = dot(tok_2[(x + d) % 4], mine).astype(BF16)
            cross[p, part, d] = remote(
                s2.at[p, d - 1, :, span],
                r2.at[p, d - 1, :, span],
                x_send.at[p, part, d - 1],
                x_recv.at[p, part, d - 1],
                x_peer[d],
            )
            cross[p, part, d].start()
        acc[p, 0:96, lanes] = dot(tok_2[x], mine)

    stages = [(0, 0), (1, 0), (0, 1), (2, 0), (1, 1), (2, 1)]

    def stage_of(n):
        return stages.index((n % 384 // 128, min(n // 384, 1)))

    def cross_sum(p, part):
        lanes = slice(128, 384) if part else slice(0, 128)
        for d in (1, 3, 2):
            cross[p, part, d].wait_recv()
        total = acc[p, 0:96, lanes]
        for d in range(3):
            total += r2[p, d, :, lanes].astype(F32)
        acc[p, 0:96, lanes] = total
        for n in (1, 2) if part else (0,):
            low = 384 * n + 128 * p
            acc_t[low : low + 128] = acc[p, :, 128 * n : 128 * n + 128].T
        for s in range(64):
            if max(stage_of(18 * s + i) for i in range(18)) == stages.index((p, part)):
                ya[s // 8, 10 * (s % 8) : 10 * (s % 8) + 10] = acc_t[18 * s : 18 * s + 10]
                zb[s % 8, 8 * (s // 8) : 8 * (s // 8) + 8] = acc_t[18 * s + 10 : 18 * s + 18]

    pass_on(0)
    pass_on(1)
    pass_core(0)
    pass_on(2)
    for s in range(8):
        halo[s].wait_recv()
    project(0)
    pass_core(1)
    attend(0)
    project(1)
    pass_core(2)
    attend(1)
    project(2)
    attend(2)
    write_att = pltpu.make_async_copy(att_ref, att_hbm, out_sem.at[0])
    write_att.start()
    acc[:, 96:128, :] = jnp.zeros((3, 32, 384), F32)
    ta[80:88] = jnp.zeros((8, 128), F32)
    tokens_out.wait_recv()
    finish(0)
    cross_send(0, 0)
    cross_send(1, 0)
    finish(1)
    cross_send(0, 1)
    cross_send(2, 0)
    cross_send(1, 1)
    finish(2)
    cross_sum(0, 0)
    cross_sum(1, 0)
    cross_send(2, 1)
    grad_tokens = dot_nt(gq[0, 0:256], wp[0]) + dot_nt(gq[1, 0:256], wp[1]) + dot_nt(gq[2, 0:256], wp[2])
    gtok_ref[...] = grad_tokens.astype(BF16)
    write_gtok = pltpu.make_async_copy(gtok_ref, gtok_hbm, out_sem.at[1])
    write_gtok.start()
    cross_sum(0, 1)
    cross_sum(2, 0)
    cross_sum(1, 1)
    cross_sum(2, 1)

    sya[...] = ya[...].astype(BF16)
    szb[...] = zb[...].astype(BF16)
    last = {}
    order = (4, 3, 5, 2, 6, 1, 7)
    for d in order:
        last["ya", d] = remote(
            sya.at[(y + d) % 8], rya.at[d - 1], ya_send.at[d - 1], ya_recv.at[d - 1], y_peer[d]
        )
        last["zb", d] = remote(
            szb.at[(z + d) % 8], rzb.at[d - 1], zb_send.at[d - 1], zb_recv.at[d - 1], z_peer[d]
        )
        last["ya", d].start()
        last["zb", d].start()
    total = zb[z]
    for d in reversed(order):
        last["zb", d].wait_recv()
        total += rzb[d - 1].astype(F32)
    for n in range(8):
        tb[n] = total[8 * n : 8 * n + 8]
    for d in order:
        last["yb", d] = remote(
            tb.at[(y + d) % 8], ryb.at[d - 1], yb_send.at[d - 1], yb_recv.at[d - 1], y_peer[d]
        )
        last["yb", d].start()
    total = ya[y]
    for d in reversed(order):
        last["ya", d].wait_recv()
        total += rya[d - 1].astype(F32)
    ta[0:80] = total
    for n in range(8):
        sza[n] = ta[10 * n : 10 * n + 16]
    for d in order:
        last["za", d] = remote(
            sza.at[(z + d) % 8], rza.at[d - 1], za_send.at[d - 1], za_recv.at[d - 1], z_peer[d]
        )
        last["za", d].start()
    total_b = tb[y]
    for d in reversed(order):
        last["yb", d].wait_recv()
        total_b += ryb[d - 1]
    total_a = sza[z]
    for d in reversed(order):
        last["za", d].wait_recv()
        total_a += rza[d - 1]
    fin[0:16] = total_a * (1.0 / 8.0)
    fin[10:18] = total_b * (1.0 / 8.0)
    out_ref[...] = fin[0:18, 0:96]

    started = list(wx.values()) + list(wc.values()) + list(halo.values()) + list(back.values())
    started += list(core.values()) + list(cross.values()) + list(last.values()) + [tokens_out]
    for copy in started:
        copy.wait_send()
    write_att.wait()
    write_gtok.wait()


def local(tokens, w_qkv, score_scale, grad_out):
    dma = pltpu.SemaphoreType.DMA
    vmem = pl.BlockSpec(memory_space=pltpu.VMEM)
    anywhere = pl.BlockSpec(memory_space=pl.ANY)
    shapes = (
        jax.ShapeDtypeStruct((256, 384), BF16),
        jax.ShapeDtypeStruct((256, 768), BF16),
        jax.ShapeDtypeStruct((18, 96), F32),
    )
    attended, grad_tokens, weight_grad = pl.pallas_call(
        kernel,
        out_shape=shapes,
        in_specs=[anywhere] * 4,
        out_specs=(anywhere, anywhere, vmem),
        scratch_shapes=[
            pltpu.VMEM((512, 768), BF16),
            pltpu.VMEM((256, 384), BF16),
            pltpu.SMEM((6,), F32),
            pltpu.VMEM((256, 384), BF16),
            pltpu.VMEM((256, 768), BF16),
            pltpu.VMEM((3, 768, 384), BF16),
            pltpu.VMEM((4, 2, 96, 256), BF16),
            pltpu.VMEM((4, 96, 512), BF16),
            pltpu.VMEM((512, 256), F32),
            pltpu.VMEM((256, 256), BF16),
            pltpu.VMEM((256, 256), BF16),
            pltpu.VMEM((3, 256, 256), BF16),
            pltpu.VMEM((3, 256, 256), F32),
            pltpu.VMEM((3, 2, 256, 128), BF16),
            pltpu.VMEM((3, 2, 256, 128), BF16),
            pltpu.VMEM((3, 512, 256), BF16),
            pltpu.VMEM((256, 768), BF16),
            pltpu.VMEM((3, 256, 256), F32),
            pltpu.VMEM((3, 256, 256), BF16),
            pltpu.VMEM((3, 256, 256), BF16),
            pltpu.VMEM((3, 512, 384), BF16),
            pltpu.VMEM((3, 3, 96, 384), BF16),
            pltpu.VMEM((3, 3, 96, 384), BF16),
            pltpu.VMEM((3, 128, 384), F32),
            pltpu.VMEM((1152, 128), F32),
            pltpu.VMEM((8, 80, 128), F32),
            pltpu.VMEM((8, 64, 128), F32),
            pltpu.VMEM((8, 80, 128), BF16),
            pltpu.VMEM((8, 64, 128), BF16),
            pltpu.VMEM((7, 80, 128), BF16),
            pltpu.VMEM((7, 64, 128), BF16),
            pltpu.VMEM((88, 128), F32),
            pltpu.VMEM((8, 8, 128), F32),
            pltpu.VMEM((8, 16, 128), F32),
            pltpu.VMEM((7, 16, 128), F32),
            pltpu.VMEM((7, 8, 128), F32),
            pltpu.VMEM((24, 128), F32),
            dma((3,)), dma((3, 3)), dma((2,)), dma((3, 4)), dma((3, 4)), dma((3, 5)), dma((3, 5)),
            dma((8,)), dma((8,)), dma((3, 8)), dma((3, 8)),
            dma, dma, dma((3, 2)), dma((3, 2)), dma((3, 2, 3)), dma((3, 2, 3)),
            dma((7,)), dma((7,)), dma((7,)), dma((7,)), dma((7,)), dma((7,)), dma((7,)), dma((7,)),
        ],
        compiler_params=pltpu.CompilerParams(
            collective_id=0, has_side_effects=True, vmem_limit_bytes=63 * 1024 * 1024
        ),
    )(tokens.reshape(256, 768), w_qkv, score_scale, grad_out.reshape(256, 384))
    return (
        attended.reshape(1, 1, 16, 16, 384),
        grad_tokens.reshape(1, 1, 16, 16, 768),
        weight_grad.T,
    )


def solution(mesh):
    return jax.shard_map(
        local,
        mesh=mesh,
        in_specs=(
            P("img", "sp", None, None, None),
            P("img", None),
            P(),
            P("img", "sp", None, None, None),
        ),
        out_specs=(
            P("img", "sp", None, None, None),
            P("img", "sp", None, None, None),
            P("img", "sp"),
        ),
        check_vma=False,
    )
```

```python
import jax
import jax.numpy as jnp
from jax import lax
from jax.experimental import pallas as pl
from jax.experimental.pallas import tpu as pltpu
from jax.sharding import PartitionSpec as P

MESH = pl.DeviceIdType.MESH
BF16 = jnp.bfloat16
F32 = jnp.float32
NORM_EPS = 1e-06
NEVER = -1e30
STRIPS = (
    (-1, 0, 0, 48),
    (1, 0, 48, 48),
    (0, -1, 96, 48),
    (0, 1, 144, 48),
    (-1, -1, 192, 16),
    (-1, 1, 208, 16),
    (1, -1, 224, 16),
    (1, 1, 240, 16),
)


def remote(src, dst, send, recv, device):
    return pltpu.make_async_remote_copy(
        src_ref=src,
        dst_ref=dst,
        send_sem=send,
        recv_sem=recv,
        device_id=device,
        device_id_type=MESH,
    )


def dot(a, b):
    return jnp.dot(a, b, preferred_element_type=F32)


def dot_nt(a, b):
    return lax.dot_general(a, b, (((1,), (1,)), ((), ())), preferred_element_type=F32)


def halo_place(j):
    strip = (j >= 48).astype(jnp.int32) + (j >= 96).astype(jnp.int32) + (j >= 144).astype(jnp.int32)
    m = j - 48 * strip
    edge = m >> 4
    along = m & 15
    low = jnp.where((strip & 1) == 0, -3, 16)
    step = jnp.where((strip & 1) == 0, -1, 1)
    level = strip < 2
    row_e = jnp.where(level, low + edge, along)
    col_e = jnp.where(level, along, low + edge)
    rstep_e = jnp.where(level, step, 0)
    cstep_e = jnp.where(level, 0, step)
    k = j - 192
    corner = k >> 4
    n = k & 15
    r3 = n >> 2
    c3 = n & 3
    rstep_c = jnp.where((corner & 2) == 0, -1, 1)
    cstep_c = jnp.where((corner & 1) == 0, -1, 1)
    row_c = jnp.where(rstep_c < 0, -3, 16) + r3
    col_c = jnp.where(cstep_c < 0, -3, 16) + c3
    is_edge = j < 192
    row = jnp.where(is_edge, row_e, row_c)
    col = jnp.where(is_edge, col_e, col_c)
    rstep = jnp.where(is_edge, rstep_e, rstep_c)
    cstep = jnp.where(is_edge, cstep_e, cstep_c)
    filled = is_edge | ((r3 < 3) & (c3 < 3))
    return row, col, rstep, cstep, filled


def owner_token(j):
    row, col, rstep, cstep, filled = halo_place(j)
    return jnp.where(filled, (row - 16 * rstep) * 16 + (col - 16 * cstep), -1)


def kernel(
    tok_hbm, w_hbm, scale_hbm, g_hbm, att_hbm, gtok_hbm, out_ref,
    tokx, g_ref, scale_ref, att_ref, gtok_ref, wp, tok_t, tok_2, bias, pack, unpack, qk, inv, qum, gm, kvx, hs, own,
    ghs, ghr, gq, s2, r2, acc, acc_t, ya, zb, sya, szb, rya, rzb, ta, tb, sza, rza, ryb, fin,
    in_sem, w_sem, out_sem, wx_send, wx_recv, wc_send, wc_recv, h_send, h_recv, gh_send, gh_recv,
    tok_send, tok_recv, core_send, core_recv, x_send, x_recv, ya_send, ya_recv, zb_send, zb_recv,
    za_send, za_recv, yb_send, yb_recv,
):
    img = lax.axis_index("img")
    sp = lax.axis_index("sp")
    x, c = img // 2, img % 2
    y, z = sp // 8, sp % 8
    other_core = (2 * x + 1 - c, sp)
    x_peer = [((2 * ((x + d) % 4) + c), sp) for d in range(4)]
    y_peer = [(img, 8 * ((y + d) % 8) + z) for d in range(8)]
    z_peer = [(img, 8 * y + (z + d) % 8) for d in range(8)]

    def tile_at(rstep, cstep):
        return (img, 8 * ((y + rstep + 8) % 8) + (z + cstep + 8) % 8)

    def block(b):
        return pl.ds(pl.multiple_of(96 * b, 32), 96)

    loads = [
        pltpu.make_async_copy(tok_hbm, tokx.at[pl.ds(0, 256)], in_sem.at[0]),
        pltpu.make_async_copy(g_hbm, g_ref, in_sem.at[1]),
        pltpu.make_async_copy(scale_hbm, scale_ref, in_sem.at[2]),
    ]
    w_loads = [
        pltpu.make_async_copy(
            w_hbm.at[:, pl.ds(384 * part + 128 * p, 128)],
            wp.at[p, block(img), pl.ds(128 * part, 128)],
            w_sem.at[p, part],
        )
        for p in range(3)
        for part in range(3)
    ]
    barrier = pltpu.get_barrier_semaphore()
    peers = [other_core] + x_peer[1:] + y_peer[1:] + z_peer[1:]
    peers += [tile_at(r, s) for r in (-1, 1) for s in (-1, 1)]
    for peer in peers[:4]:
        pl.semaphore_signal(barrier, inc=1, device_id=peer, device_id_type=MESH)
    for load in w_loads + loads[:1]:
        load.start()
    for peer in peers[4:]:
        pl.semaphore_signal(barrier, inc=1, device_id=peer, device_id_type=MESH)
    for load in loads[1:]:
        load.start()

    for load in w_loads:
        load.wait()
    pl.semaphore_wait(barrier, len(peers))

    wx, wc = {}, {}

    def to_core(p, n, ref):
        wc[p, n] = remote(ref, ref, wc_send.at[p, n], wc_recv.at[p, n], other_core)
        wc[p, n].start()

    def to_x(p, n, ref, d):
        wx[p, n] = remote(ref, ref, wx_send.at[p, n], wx_recv.at[p, n], x_peer[d])
        wx[p, n].start()

    def half(b, h):
        return pl.ds(pl.multiple_of(96 * b + 48 * h, 16), 48)

    left, right, across = [2 * ((x + d) % 4) + c for d in (3, 1, 2)]

    def share(p):
        mine = wp.at[p, block(img)]
        to_x(p, 2, mine, 2)
        to_x(p, 0, mine, 1)
        to_x(p, 1, mine, 3)
        to_core(p, 0, mine)

    def pass_on(p):
        wx[p, 0].wait_recv()
        to_core(p, 1, wp.at[p, block(left)])
        wx[p, 1].wait_recv()
        to_core(p, 2, wp.at[p, block(right)])

    def pass_core(p):
        wx[p, 2].wait_recv()
        to_core(p, 3, wp.at[p, block(across)])

    for p in range(3):
        share(p)

    j_rows = lax.broadcasted_iota(jnp.int32, (256, 1), 0)
    j_cols = lax.broadcasted_iota(jnp.int32, (1, 256), 1)
    wide_rows = lax.broadcasted_iota(jnp.int32, (256, 256), 0)
    wide_cols = lax.broadcasted_iota(jnp.int32, (256, 256), 1)
    pack[...] = jnp.where(owner_token(j_rows) == wide_cols, 1.0, 0.0).astype(BF16)

    for load in loads:
        load.wait()
    hs[...] = dot(pack[...], tokx[0:256]).astype(BF16)
    halo = {}
    for s, (rstep, cstep, first, rows) in reversed(list(enumerate(STRIPS))):
        halo[s] = remote(
            hs.at[pl.ds(first, rows)],
            tokx.at[pl.ds(256 + first, rows)],
            h_send.at[s],
            h_recv.at[s],
            tile_at(-rstep, -cstep),
        )
        halo[s].start()

    query = lax.broadcasted_iota(jnp.int32, (1, 256), 1)
    query_row, query_col = query >> 4, query & 15

    def put_bias(low, key_row, key_col):
        near = (jnp.abs(key_row - query_row) <= 3) & (jnp.abs(key_col - query_col) <= 3)
        bias[low : low + 256] = jnp.where(near, 0.0, NEVER).astype(F32)

    put_bias(0, j_rows >> 4, j_rows & 15)
    row, col, _, _, filled = halo_place(j_rows)
    grow, gcol = row + 16 * y, col + 16 * z
    inside = filled & (grow >= 0) & (grow < 128) & (gcol >= 0) & (gcol < 128)
    put_bias(256, jnp.where(inside, row, 1000), col)
    unpack[...] = jnp.where(owner_token(j_cols) == wide_rows, 1.0, 0.0).astype(BF16)
    lane_r = lax.broadcasted_iota(jnp.int32, (128, 128), 0)
    lane_c = lax.broadcasted_iota(jnp.int32, (128, 128), 1)
    same_head = jnp.where((lane_r >> 6) == (lane_c >> 6), 1.0, 0.0).astype(BF16)
    eye = jnp.where(lane_r == lane_c, 1.0, 0.0).astype(BF16)
    lane = lax.broadcasted_iota(jnp.int32, (1, 128), 1)
    head_mask = [jnp.where((lane >> 6) == e, 1.0, 0.0).astype(F32) for e in range(2)]

    for p in range(3):
        g_pair = g_ref[:, 128 * p : 128 * p + 128].astype(F32)
        for e in range(2):
            gm[p, e] = (g_pair * head_mask[e]).astype(BF16)

    for b in range(8):
        tok_t[b // 2, b % 2] = tokx[0:256, 96 * b : 96 * b + 96].astype(F32).T.astype(BF16)
    tokens_out = remote(
        tok_t.at[:, 1 - c], tok_2.at[:, :, pl.ds(256, 256)], tok_send, tok_recv, other_core
    )
    tokens_out.start()
    tok_2[:, :, 0:256] = tok_t[:, c]
    acc[:, 96:128, :] = jnp.zeros((3, 32, 384), F32)
    ta[80:88] = jnp.zeros((8, 128), F32)

    def head_sum(v):
        high = v.astype(BF16)
        low = (v - high.astype(F32)).astype(BF16)
        return dot(high, same_head) + dot(low, same_head)

    back, core, cross = {}, {}, {}

    def exchange(p, n, lanes):
        core[p, n] = remote(
            gq.at[p, pl.ds(0, 256), lanes],
            gq.at[p, pl.ds(256, 256), lanes],
            core_send.at[p, n],
            core_recv.at[p, n],
            other_core,
        )
        core[p, n].start()

    def project(p):
        for d in range(4):
            wc[p, d].wait_recv()
        low = dot(tokx[0:256], wp[p]).astype(BF16)
        far = dot(tokx[256:512], wp[p, :, 128:384]).astype(BF16)
        qk[p] = low[:, 0:256]
        q = low[:, 0:128].astype(F32)
        k = low[:, 128:256].astype(F32)
        k_far = far[:, 0:128].astype(F32)
        inv_q = lax.rsqrt(head_sum(q * q) * (1.0 / 64.0) + NORM_EPS) * 0.125
        inv_k = lax.rsqrt(head_sum(k * k) * (1.0 / 64.0) + NORM_EPS) * 0.125
        inv_far = lax.rsqrt(head_sum(k_far * k_far) * (1.0 / 64.0) + NORM_EPS) * 0.125
        inv[p, :, 0:128] = inv_q
        inv[p, :, 128:256] = inv_k
        q_unit = q * inv_q
        for e in range(2):
            qum[p, e] = (q_unit * head_mask[e]).astype(BF16)
        kvx[p, 0:256, 0:128] = (k * inv_k).astype(BF16)
        kvx[p, 0:256, 128:256] = low[:, 256:384]
        kvx[p, 256:512, 0:128] = (k_far * inv_far).astype(BF16)
        kvx[p, 256:512, 128:256] = far[:, 128:256]

    def attend(p):
        key = kvx[p, :, 0:128]
        value = kvx[p, :, 128:256]
        lows, grads = [], []
        for e in range(2):
            scale = scale_ref[2 * p + e]
            raised = jnp.exp(dot_nt(key, qum[p, e]) * scale + bias[...])
            attention = raised * (1.0 / jnp.sum(raised, axis=0, keepdims=True))
            grad_att = dot_nt(value, gm[p, e])
            row_total = jnp.sum(attention * grad_att, axis=0, keepdims=True)
            lows.append(attention.astype(BF16))
            grads.append((attention * scale * (grad_att - row_total)).astype(BF16))

        def key_side(first):
            rows = slice(first, first + 256)
            grad_k = dot(grads[0][rows], qum[p, 0]) + dot(grads[1][rows], qum[p, 1])
            grad_v = dot(lows[0][rows], gm[p, 0]) + dot(lows[1][rows], gm[p, 1])
            return grad_k, grad_v

        grad_k, grad_v = key_side(256)
        ghs[p, :, 0:128] = grad_k.astype(BF16)
        ghs[p, :, 128:256] = grad_v.astype(BF16)
        for s, (rstep, cstep, first, rows) in reversed(list(enumerate(STRIPS))):
            span = pl.ds(first, rows)
            back[p, s] = remote(
                ghs.at[p, span], ghr.at[p, span], gh_send.at[p, s], gh_recv.at[p, s], tile_at(rstep, cstep)
            )
            back[p, s].start()
        key_t = dot_nt(eye, key).astype(BF16)
        value_t = dot_nt(eye, value).astype(BF16)
        att_t, gq_t = [], []
        for e in range(2):
            rows = slice(64 * e, 64 * e + 64)
            gq_t.append(dot(key_t[rows], grads[e]))
            att_t.append(dot(value_t[rows], lows[e]))
        grad_q = jnp.concatenate(gq_t, axis=0).T
        q = qk[p, :, 0:128].astype(F32)
        inv_q = inv[p, :, 0:128]
        gq[p, 0:256, 0:128] = (inv_q * (grad_q - q * (inv_q * inv_q) * head_sum(grad_q * q))).astype(BF16)
        exchange(p, 0, pl.ds(0, 128))
        grad_k, grad_v = key_side(0)
        own[p, :, 0:128] = grad_k
        own[p, :, 128:256] = grad_v
        att_ref[:, 128 * p : 128 * p + 128] = jnp.concatenate(att_t, axis=0).T.astype(BF16)

    def finish(p):
        for s in range(8):
            back[p, s].wait_recv()
        grad_kv = own[p] + dot(unpack[...], ghr[p])
        grad_k = grad_kv[:, 0:128]
        k = qk[p, :, 128:256].astype(F32)
        inv_k = inv[p, :, 128:256]
        gq[p, 0:256, 128:256] = (inv_k * (grad_k - k * (inv_k * inv_k) * head_sum(grad_k * k))).astype(BF16)
        gq[p, 0:256, 256:384] = grad_kv[:, 128:256].astype(BF16)
        exchange(p, 1, pl.ds(128, 256))

    def cross_send(p, part):
        core[p, part].wait_recv()
        lanes = slice(128, 384) if part else slice(0, 128)
        span = pl.ds(128, 256) if part else pl.ds(0, 128)
        mine = gq[p, :, lanes]
        for d in (2, 1, 3):
            s2[p, d - 1, :, lanes] = dot(tok_2[(x + d) % 4], mine).astype(BF16)
            cross[p, part, d] = remote(
                s2.at[p, d - 1, :, span],
                r2.at[p, d - 1, :, span],
                x_send.at[p, part, d - 1],
                x_recv.at[p, part, d - 1],
                x_peer[d],
            )
            cross[p, part, d].start()
        acc[p, 0:96, lanes] = dot(tok_2[x], mine)

    stages = [(0, 0), (1, 0), (0, 1), (2, 0), (1, 1), (2, 1)]

    def stage_of(n):
        return stages.index((n % 384 // 128, min(n // 384, 1)))

    def cross_sum(p, part):
        lanes = slice(128, 384) if part else slice(0, 128)
        for d in (1, 3, 2):
            cross[p, part, d].wait_recv()
        total = acc[p, 0:96, lanes]
        for d in range(3):
            total += r2[p, d, :, lanes].astype(F32)
        acc[p, 0:96, lanes] = total
        for n in (1, 2) if part else (0,):
            low = 384 * n + 128 * p
            acc_t[low : low + 128] = acc[p, :, 128 * n : 128 * n + 128].T
        for s in range(64):
            if max(stage_of(18 * s + i) for i in range(18)) == stages.index((p, part)):
                ya[s // 8, 10 * (s % 8) : 10 * (s % 8) + 10] = acc_t[18 * s : 18 * s + 10]
                zb[s % 8, 8 * (s // 8) : 8 * (s // 8) + 8] = acc_t[18 * s + 10 : 18 * s + 18]

    pass_on(0)
    pass_core(0)
    for s in range(8):
        halo[s].wait_recv()
    project(0)
    attend(0)
    pass_on(1)
    pass_core(1)
    project(1)
    tokens_out.wait_recv()
    cross_send(0, 0)
    attend(1)
    pass_on(2)
    pass_core(2)
    finish(0)
    cross_send(1, 0)
    project(2)
    attend(2)
    write_att = pltpu.make_async_copy(att_ref, att_hbm, out_sem.at[0])
    write_att.start()
    cross_send(0, 1)
    finish(1)
    cross_send(2, 0)
    cross_send(1, 1)
    finish(2)
    cross_sum(0, 0)
    cross_sum(1, 0)
    cross_send(2, 1)
    grad_tokens = dot_nt(gq[0, 0:256], wp[0]) + dot_nt(gq[1, 0:256], wp[1]) + dot_nt(gq[2, 0:256], wp[2])
    gtok_ref[...] = grad_tokens.astype(BF16)
    write_gtok = pltpu.make_async_copy(gtok_ref, gtok_hbm, out_sem.at[1])
    write_gtok.start()
    cross_sum(0, 1)
    cross_sum(2, 0)
    cross_sum(1, 1)
    cross_sum(2, 1)

    sya[...] = ya[...].astype(BF16)
    szb[...] = zb[...].astype(BF16)
    last = {}
    order = (4, 3, 5, 2, 6, 1, 7)
    for d in order:
        last["ya", d] = remote(
            sya.at[(y + d) % 8], rya.at[d - 1], ya_send.at[d - 1], ya_recv.at[d - 1], y_peer[d]
        )
        last["zb", d] = remote(
            szb.at[(z + d) % 8], rzb.at[d - 1], zb_send.at[d - 1], zb_recv.at[d - 1], z_peer[d]
        )
        last["ya", d].start()
        last["zb", d].start()
    total = zb[z]
    for d in reversed(order):
        last["zb", d].wait_recv()
        total += rzb[d - 1].astype(F32)
    for n in range(8):
        tb[n] = total[8 * n : 8 * n + 8]
    for d in order:
        last["yb", d] = remote(
            tb.at[(y + d) % 8], ryb.at[d - 1], yb_send.at[d - 1], yb_recv.at[d - 1], y_peer[d]
        )
        last["yb", d].start()
    total = ya[y]
    for d in reversed(order):
        last["ya", d].wait_recv()
        total += rya[d - 1].astype(F32)
    ta[0:80] = total
    for n in range(8):
        sza[n] = ta[10 * n : 10 * n + 16]
    for d in order:
        last["za", d] = remote(
            sza.at[(z + d) % 8], rza.at[d - 1], za_send.at[d - 1], za_recv.at[d - 1], z_peer[d]
        )
        last["za", d].start()
    total_b = tb[y]
    for d in reversed(order):
        last["yb", d].wait_recv()
        total_b += ryb[d - 1]
    total_a = sza[z]
    for d in reversed(order):
        last["za", d].wait_recv()
        total_a += rza[d - 1]
    fin[0:16] = total_a * (1.0 / 8.0)
    fin[10:18] = total_b * (1.0 / 8.0)
    out_ref[...] = fin[0:18, 0:96]

    started = list(wx.values()) + list(wc.values()) + list(halo.values()) + list(back.values())
    started += list(core.values()) + list(cross.values()) + list(last.values()) + [tokens_out]
    for copy in started:
        copy.wait_send()
    write_att.wait()
    write_gtok.wait()


def local(tokens, w_qkv, score_scale, grad_out):
    dma = pltpu.SemaphoreType.DMA
    vmem = pl.BlockSpec(memory_space=pltpu.VMEM)
    anywhere = pl.BlockSpec(memory_space=pl.ANY)
    shapes = (
        jax.ShapeDtypeStruct((256, 384), BF16),
        jax.ShapeDtypeStruct((256, 768), BF16),
        jax.ShapeDtypeStruct((18, 96), F32),
    )
    attended, grad_tokens, weight_grad = pl.pallas_call(
        kernel,
        out_shape=shapes,
        in_specs=[anywhere] * 4,
        out_specs=(anywhere, anywhere, vmem),
        scratch_shapes=[
            pltpu.VMEM((512, 768), BF16),
            pltpu.VMEM((256, 384), BF16),
            pltpu.SMEM((6,), F32),
            pltpu.VMEM((256, 384), BF16),
            pltpu.VMEM((256, 768), BF16),
            pltpu.VMEM((3, 768, 384), BF16),
            pltpu.VMEM((4, 2, 96, 256), BF16),
            pltpu.VMEM((4, 96, 512), BF16),
            pltpu.VMEM((512, 256), F32),
            pltpu.VMEM((256, 256), BF16),
            pltpu.VMEM((256, 256), BF16),
            pltpu.VMEM((3, 256, 256), BF16),
            pltpu.VMEM((3, 256, 256), F32),
            pltpu.VMEM((3, 2, 256, 128), BF16),
            pltpu.VMEM((3, 2, 256, 128), BF16),
            pltpu.VMEM((3, 512, 256), BF16),
            pltpu.VMEM((256, 768), BF16),
            pltpu.VMEM((3, 256, 256), F32),
            pltpu.VMEM((3, 256, 256), BF16),
            pltpu.VMEM((3, 256, 256), BF16),
            pltpu.VMEM((3, 512, 384), BF16),
            pltpu.VMEM((3, 3, 96, 384), BF16),
            pltpu.VMEM((3, 3, 96, 384), BF16),
            pltpu.VMEM((3, 128, 384), F32),
            pltpu.VMEM((1152, 128), F32),
            pltpu.VMEM((8, 80, 128), F32),
            pltpu.VMEM((8, 64, 128), F32),
            pltpu.VMEM((8, 80, 128), BF16),
            pltpu.VMEM((8, 64, 128), BF16),
            pltpu.VMEM((7, 80, 128), BF16),
            pltpu.VMEM((7, 64, 128), BF16),
            pltpu.VMEM((88, 128), F32),
            pltpu.VMEM((8, 8, 128), F32),
            pltpu.VMEM((8, 16, 128), F32),
            pltpu.VMEM((7, 16, 128), F32),
            pltpu.VMEM((7, 8, 128), F32),
            pltpu.VMEM((24, 128), F32),
            dma((3,)), dma((3, 3)), dma((2,)), dma((3, 3)), dma((3, 3)), dma((3, 4)), dma((3, 4)),
            dma((8,)), dma((8,)), dma((3, 8)), dma((3, 8)),
            dma, dma, dma((3, 2)), dma((3, 2)), dma((3, 2, 3)), dma((3, 2, 3)),
            dma((7,)), dma((7,)), dma((7,)), dma((7,)), dma((7,)), dma((7,)), dma((7,)), dma((7,)),
        ],
        compiler_params=pltpu.CompilerParams(
            collective_id=0, has_side_effects=True, vmem_limit_bytes=63 * 1024 * 1024
        ),
    )(tokens.reshape(256, 768), w_qkv, score_scale, grad_out.reshape(256, 384))
    return (
        attended.reshape(1, 1, 16, 16, 384),
        grad_tokens.reshape(1, 1, 16, 16, 768),
        weight_grad.T,
    )


def solution(mesh):
    return jax.shard_map(
        local,
        mesh=mesh,
        in_specs=(
            P("img", "sp", None, None, None),
            P("img", None),
            P(),
            P("img", "sp", None, None, None),
        ),
        out_specs=(
            P("img", "sp", None, None, None),
            P("img", "sp", None, None, None),
            P("img", "sp"),
        ),
        check_vma=False,
    )
```

```python
import jax
import jax.numpy as jnp
from jax import lax
from jax.experimental import pallas as pl
from jax.experimental.pallas import tpu as pltpu
from jax.sharding import PartitionSpec as P

MESH = pl.DeviceIdType.MESH
BF16 = jnp.bfloat16
F32 = jnp.float32
NORM_EPS = 1e-06
NEVER = -1e30
STRIPS = (
    (-1, 0, 0, 48),
    (1, 0, 48, 48),
    (0, -1, 96, 48),
    (0, 1, 144, 48),
    (-1, -1, 192, 16),
    (-1, 1, 208, 16),
    (1, -1, 224, 16),
    (1, 1, 240, 16),
)


def remote(src, dst, send, recv, device):
    return pltpu.make_async_remote_copy(
        src_ref=src,
        dst_ref=dst,
        send_sem=send,
        recv_sem=recv,
        device_id=device,
        device_id_type=MESH,
    )


def dot(a, b):
    return jnp.dot(a, b, preferred_element_type=F32)


def dot_nt(a, b):
    return lax.dot_general(a, b, (((1,), (1,)), ((), ())), preferred_element_type=F32)


def halo_place(j):
    strip = (j >= 48).astype(jnp.int32) + (j >= 96).astype(jnp.int32) + (j >= 144).astype(jnp.int32)
    m = j - 48 * strip
    edge = m >> 4
    along = m & 15
    low = jnp.where((strip & 1) == 0, -3, 16)
    step = jnp.where((strip & 1) == 0, -1, 1)
    level = strip < 2
    row_e = jnp.where(level, low + edge, along)
    col_e = jnp.where(level, along, low + edge)
    rstep_e = jnp.where(level, step, 0)
    cstep_e = jnp.where(level, 0, step)
    k = j - 192
    corner = k >> 4
    n = k & 15
    r3 = n >> 2
    c3 = n & 3
    rstep_c = jnp.where((corner & 2) == 0, -1, 1)
    cstep_c = jnp.where((corner & 1) == 0, -1, 1)
    row_c = jnp.where(rstep_c < 0, -3, 16) + r3
    col_c = jnp.where(cstep_c < 0, -3, 16) + c3
    is_edge = j < 192
    row = jnp.where(is_edge, row_e, row_c)
    col = jnp.where(is_edge, col_e, col_c)
    rstep = jnp.where(is_edge, rstep_e, rstep_c)
    cstep = jnp.where(is_edge, cstep_e, cstep_c)
    filled = is_edge | ((r3 < 3) & (c3 < 3))
    return row, col, rstep, cstep, filled


def owner_token(j):
    row, col, rstep, cstep, filled = halo_place(j)
    return jnp.where(filled, (row - 16 * rstep) * 16 + (col - 16 * cstep), -1)


def kernel(
    tok_hbm, w_hbm, scale_hbm, g_hbm, att_hbm, gtok_hbm, out_ref,
    tokx, g_ref, scale_ref, att_ref, gtok_ref, wp, tok_t, tok_2, bias, pack, unpack, qk, inv, qum, gm, kvx, hs, own,
    ghs, ghr, gq, s2, r2, acc, acc_t, ya, zb, sya, szb, rya, rzb, ta, tb, sza, rza, ryb, fin,
    in_sem, w_sem, out_sem, wx_send, wx_recv, wc_send, wc_recv, h_send, h_recv, gh_send, gh_recv,
    tok_send, tok_recv, core_send, core_recv, x_send, x_recv, ya_send, ya_recv, zb_send, zb_recv,
    za_send, za_recv, yb_send, yb_recv,
):
    img = lax.axis_index("img")
    sp = lax.axis_index("sp")
    x, c = img // 2, img % 2
    y, z = sp // 8, sp % 8
    other_core = (2 * x + 1 - c, sp)
    x_peer = [((2 * ((x + d) % 4) + c), sp) for d in range(4)]
    y_peer = [(img, 8 * ((y + d) % 8) + z) for d in range(8)]
    z_peer = [(img, 8 * y + (z + d) % 8) for d in range(8)]

    def tile_at(rstep, cstep):
        return (img, 8 * ((y + rstep + 8) % 8) + (z + cstep + 8) % 8)

    def block(b):
        return pl.ds(pl.multiple_of(96 * b, 32), 96)

    loads = [
        pltpu.make_async_copy(tok_hbm, tokx.at[pl.ds(0, 256)], in_sem.at[0]),
        pltpu.make_async_copy(g_hbm, g_ref, in_sem.at[1]),
        pltpu.make_async_copy(scale_hbm, scale_ref, in_sem.at[2]),
    ]
    w_loads = [
        pltpu.make_async_copy(
            w_hbm.at[:, pl.ds(384 * part + 128 * p, 128)],
            wp.at[p, block(img), pl.ds(128 * part, 128)],
            w_sem.at[p, part],
        )
        for p in range(3)
        for part in range(3)
    ]
    barrier = pltpu.get_barrier_semaphore()
    peers = [other_core] + x_peer[1:] + y_peer[1:] + z_peer[1:]
    peers += [tile_at(r, s) for r in (-1, 1) for s in (-1, 1)]
    for peer in peers[:4]:
        pl.semaphore_signal(barrier, inc=1, device_id=peer, device_id_type=MESH)
    for load in w_loads + loads[:1]:
        load.start()
    for peer in peers[4:]:
        pl.semaphore_signal(barrier, inc=1, device_id=peer, device_id_type=MESH)
    for load in loads[1:]:
        load.start()

    for load in w_loads:
        load.wait()
    pl.semaphore_wait(barrier, len(peers))

    wx, wc = {}, {}

    def to_core(p, n, ref):
        wc[p, n] = remote(ref, ref, wc_send.at[p, n], wc_recv.at[p, n], other_core)
        wc[p, n].start()

    def to_x(p, n, ref, d):
        wx[p, n] = remote(ref, ref, wx_send.at[p, n], wx_recv.at[p, n], x_peer[d])
        wx[p, n].start()

    def half(b, h):
        return pl.ds(pl.multiple_of(96 * b + 48 * h, 16), 48)

    left, right, across = [2 * ((x + d) % 4) + c for d in (3, 1, 2)]

    def share(p):
        mine = wp.at[p, block(img)]
        to_x(p, 2, mine, 2)
        to_x(p, 0, mine, 1)
        to_x(p, 1, mine, 3)
        to_core(p, 0, mine)

    def pass_on(p):
        wx[p, 0].wait_recv()
        to_core(p, 1, wp.at[p, block(left)])
        wx[p, 1].wait_recv()
        to_core(p, 2, wp.at[p, block(right)])

    def pass_core(p):
        wx[p, 2].wait_recv()
        to_core(p, 3, wp.at[p, block(across)])

    for p in range(3):
        share(p)

    j_rows = lax.broadcasted_iota(jnp.int32, (256, 1), 0)
    j_cols = lax.broadcasted_iota(jnp.int32, (1, 256), 1)
    wide_rows = lax.broadcasted_iota(jnp.int32, (256, 256), 0)
    wide_cols = lax.broadcasted_iota(jnp.int32, (256, 256), 1)
    pack[...] = jnp.where(owner_token(j_rows) == wide_cols, 1.0, 0.0).astype(BF16)

    for load in loads:
        load.wait()
    hs[...] = dot(pack[...], tokx[0:256]).astype(BF16)
    halo = {}
    for s, (rstep, cstep, first, rows) in reversed(list(enumerate(STRIPS))):
        halo[s] = remote(
            hs.at[pl.ds(first, rows)],
            tokx.at[pl.ds(256 + first, rows)],
            h_send.at[s],
            h_recv.at[s],
            tile_at(-rstep, -cstep),
        )
        halo[s].start()

    query = lax.broadcasted_iota(jnp.int32, (1, 256), 1)
    query_row, query_col = query >> 4, query & 15

    def put_bias(low, key_row, key_col):
        near = (jnp.abs(key_row - query_row) <= 3) & (jnp.abs(key_col - query_col) <= 3)
        bias[low : low + 256] = jnp.where(near, 0.0, NEVER).astype(F32)

    put_bias(0, j_rows >> 4, j_rows & 15)
    row, col, _, _, filled = halo_place(j_rows)
    grow, gcol = row + 16 * y, col + 16 * z
    inside = filled & (grow >= 0) & (grow < 128) & (gcol >= 0) & (gcol < 128)
    put_bias(256, jnp.where(inside, row, 1000), col)
    unpack[...] = jnp.where(owner_token(j_cols) == wide_rows, 1.0, 0.0).astype(BF16)
    lane_r = lax.broadcasted_iota(jnp.int32, (128, 128), 0)
    lane_c = lax.broadcasted_iota(jnp.int32, (128, 128), 1)
    same_head = jnp.where((lane_r >> 6) == (lane_c >> 6), 1.0, 0.0).astype(BF16)
    eye = jnp.where(lane_r == lane_c, 1.0, 0.0).astype(BF16)
    lane = lax.broadcasted_iota(jnp.int32, (1, 128), 1)
    head_mask = [jnp.where((lane >> 6) == e, 1.0, 0.0).astype(F32) for e in range(2)]

    for p in range(3):
        g_pair = g_ref[:, 128 * p : 128 * p + 128].astype(F32)
        for e in range(2):
            gm[p, e] = (g_pair * head_mask[e]).astype(BF16)

    for b in range(8):
        tok_t[b // 2, b % 2] = tokx[0:256, 96 * b : 96 * b + 96].astype(F32).T.astype(BF16)
    tokens_out = remote(
        tok_t.at[:, 1 - c], tok_2.at[:, :, pl.ds(256, 256)], tok_send, tok_recv, other_core
    )
    tokens_out.start()
    tok_2[:, :, 0:256] = tok_t[:, c]
    acc[:, 96:128, :] = jnp.zeros((3, 32, 384), F32)
    ta[80:88] = jnp.zeros((8, 128), F32)

    def head_sum(v):
        high = v.astype(BF16)
        low = (v - high.astype(F32)).astype(BF16)
        return dot(high, same_head) + dot(low, same_head)

    back, core, cross = {}, {}, {}

    def exchange(p, n, lanes):
        core[p, n] = remote(
            gq.at[p, pl.ds(0, 256), lanes],
            gq.at[p, pl.ds(256, 256), lanes],
            core_send.at[p, n],
            core_recv.at[p, n],
            other_core,
        )
        core[p, n].start()

    def project(p):
        for d in range(4):
            wc[p, d].wait_recv()
        low = dot(tokx[0:256], wp[p]).astype(BF16)
        far = dot(tokx[256:512], wp[p, :, 128:384]).astype(BF16)
        qk[p] = low[:, 0:256]
        q = low[:, 0:128].astype(F32)
        k = low[:, 128:256].astype(F32)
        k_far = far[:, 0:128].astype(F32)
        inv_q = lax.rsqrt(head_sum(q * q) * (1.0 / 64.0) + NORM_EPS) * 0.125
        inv_k = lax.rsqrt(head_sum(k * k) * (1.0 / 64.0) + NORM_EPS) * 0.125
        inv_far = lax.rsqrt(head_sum(k_far * k_far) * (1.0 / 64.0) + NORM_EPS) * 0.125
        inv[p, :, 0:128] = inv_q
        inv[p, :, 128:256] = inv_k
        q_unit = q * inv_q
        for e in range(2):
            qum[p, e] = (q_unit * head_mask[e]).astype(BF16)
        kvx[p, 0:256, 0:128] = (k * inv_k).astype(BF16)
        kvx[p, 0:256, 128:256] = low[:, 256:384]
        kvx[p, 256:512, 0:128] = (k_far * inv_far).astype(BF16)
        kvx[p, 256:512, 128:256] = far[:, 128:256]

    def attend(p):
        key = kvx[p, :, 0:128]
        value = kvx[p, :, 128:256]
        lows, grads = [], []
        for e in range(2):
            scale = scale_ref[2 * p + e]
            raised = jnp.exp(dot_nt(key, qum[p, e]) * scale + bias[...])
            attention = raised * (1.0 / jnp.sum(raised, axis=0, keepdims=True))
            grad_att = dot_nt(value, gm[p, e])
            row_total = jnp.sum(attention * grad_att, axis=0, keepdims=True)
            lows.append(attention.astype(BF16))
            grads.append((attention * scale * (grad_att - row_total)).astype(BF16))

        def key_side(first):
            rows = slice(first, first + 256)
            grad_k = dot(grads[0][rows], qum[p, 0]) + dot(grads[1][rows], qum[p, 1])
            grad_v = dot(lows[0][rows], gm[p, 0]) + dot(lows[1][rows], gm[p, 1])
            return grad_k, grad_v

        grad_k, grad_v = key_side(256)
        ghs[p, :, 0:128] = grad_k.astype(BF16)
        ghs[p, :, 128:256] = grad_v.astype(BF16)
        for s, (rstep, cstep, first, rows) in reversed(list(enumerate(STRIPS))):
            span = pl.ds(first, rows)
            back[p, s] = remote(
                ghs.at[p, span], ghr.at[p, span], gh_send.at[p, s], gh_recv.at[p, s], tile_at(rstep, cstep)
            )
            back[p, s].start()
        key_t = dot_nt(eye, key).astype(BF16)
        value_t = dot_nt(eye, value).astype(BF16)
        att_t, gq_t = [], []
        for e in range(2):
            rows = slice(64 * e, 64 * e + 64)
            gq_t.append(dot(key_t[rows], grads[e]))
            att_t.append(dot(value_t[rows], lows[e]))
        grad_q = jnp.concatenate(gq_t, axis=0).T
        q = qk[p, :, 0:128].astype(F32)
        inv_q = inv[p, :, 0:128]
        gq[p, 0:256, 0:128] = (inv_q * (grad_q - q * (inv_q * inv_q) * head_sum(grad_q * q))).astype(BF16)
        exchange(p, 0, pl.ds(0, 128))
        grad_k, grad_v = key_side(0)
        own[p, :, 0:128] = grad_k
        own[p, :, 128:256] = grad_v
        att_ref[:, 128 * p : 128 * p + 128] = jnp.concatenate(att_t, axis=0).T.astype(BF16)

    def finish(p):
        for s in range(8):
            back[p, s].wait_recv()
        grad_kv = own[p] + dot(unpack[...], ghr[p])
        grad_k = grad_kv[:, 0:128]
        k = qk[p, :, 128:256].astype(F32)
        inv_k = inv[p, :, 128:256]
        gq[p, 0:256, 128:256] = (inv_k * (grad_k - k * (inv_k * inv_k) * head_sum(grad_k * k))).astype(BF16)
        gq[p, 0:256, 256:384] = grad_kv[:, 128:256].astype(BF16)
        exchange(p, 1, pl.ds(128, 256))

    def cross_send(p, part):
        core[p, part].wait_recv()
        lanes = slice(128, 384) if part else slice(0, 128)
        span = pl.ds(128, 256) if part else pl.ds(0, 128)
        mine = gq[p, :, lanes]
        for d in (2, 1, 3):
            s2[p, d - 1, :, lanes] = dot(tok_2[(x + d) % 4], mine).astype(BF16)
            cross[p, part, d] = remote(
                s2.at[p, d - 1, :, span],
                r2.at[p, d - 1, :, span],
                x_send.at[p, part, d - 1],
                x_recv.at[p, part, d - 1],
                x_peer[d],
            )
            cross[p, part, d].start()
        acc[p, 0:96, lanes] = dot(tok_2[x], mine)

    stages = [(0, 0), (1, 0), (0, 1), (2, 0), (1, 1), (2, 1)]

    def stage_of(n):
        return stages.index((n % 384 // 128, min(n // 384, 1)))

    def cross_sum(p, part):
        lanes = slice(128, 384) if part else slice(0, 128)
        for d in (1, 3, 2):
            cross[p, part, d].wait_recv()
        total = acc[p, 0:96, lanes]
        for d in range(3):
            total += r2[p, d, :, lanes].astype(F32)
        acc[p, 0:96, lanes] = total
        for n in (1, 2) if part else (0,):
            low = 384 * n + 128 * p
            acc_t[low : low + 128] = acc[p, :, 128 * n : 128 * n + 128].T
        for s in range(64):
            if max(stage_of(18 * s + i) for i in range(18)) == stages.index((p, part)):
                ya[s // 8, 10 * (s % 8) : 10 * (s % 8) + 10] = acc_t[18 * s : 18 * s + 10]
                zb[s % 8, 8 * (s // 8) : 8 * (s // 8) + 8] = acc_t[18 * s + 10 : 18 * s + 18]

    pass_on(0)
    pass_core(0)
    for s in range(8):
        halo[s].wait_recv()
    project(0)
    attend(0)
    pass_on(1)
    pass_core(1)
    project(1)
    tokens_out.wait_recv()
    cross_send(0, 0)
    attend(1)
    pass_on(2)
    pass_core(2)
    finish(0)
    cross_send(1, 0)
    project(2)
    attend(2)
    write_att = pltpu.make_async_copy(att_ref, att_hbm, out_sem.at[0])
    write_att.start()
    cross_send(0, 1)
    finish(1)
    cross_send(2, 0)
    cross_send(1, 1)
    finish(2)
    cross_sum(0, 0)
    cross_sum(1, 0)
    cross_send(2, 1)
    grad_tokens = dot_nt(gq[0, 0:256], wp[0]) + dot_nt(gq[1, 0:256], wp[1]) + dot_nt(gq[2, 0:256], wp[2])
    gtok_ref[...] = grad_tokens.astype(BF16)
    write_gtok = pltpu.make_async_copy(gtok_ref, gtok_hbm, out_sem.at[1])
    write_gtok.start()
    cross_sum(0, 1)
    cross_sum(2, 0)
    cross_sum(1, 1)

    last = {}
    order = (4, 3, 5, 2, 6, 1, 7)
    for d in order:
        last["ya", d] = remote(
            sya.at[(y + d) % 8], rya.at[d - 1], ya_send.at[d - 1], ya_recv.at[d - 1], y_peer[d]
        )
        for h in range(2):
            rows = pl.ds(32 * h, 32)
            last["zb", h, d] = remote(
                szb.at[(z + d) % 8, rows], rzb.at[d - 1, rows], zb_send.at[h, d - 1], zb_recv.at[h, d - 1], z_peer[d]
            )

    def waits_for_last(row):
        return (row == 4) | (row == 5) | (row == 7)

    sya[0:4] = ya[0:4].astype(BF16)
    sya[6] = ya[6].astype(BF16)
    szb[:, 0:32] = zb[:, 0:32].astype(BF16)
    for d in order:
        pl.when(jnp.logical_not(waits_for_last((y + d) % 8)))(last["ya", d].start)
        last["zb", 0, d].start()
    cross_sum(2, 1)

    sya[4:6] = ya[4:6].astype(BF16)
    sya[7] = ya[7].astype(BF16)
    szb[:, 32:64] = zb[:, 32:64].astype(BF16)
    for d in order:
        pl.when(waits_for_last((y + d) % 8))(last["ya", d].start)
        last["zb", 1, d].start()
    total = zb[z]
    for d in reversed(order):
        last["zb", 0, d].wait_recv()
        last["zb", 1, d].wait_recv()
        total += rzb[d - 1].astype(F32)
    for n in range(8):
        tb[n] = total[8 * n : 8 * n + 8]
    for d in order:
        last["yb", d] = remote(
            tb.at[(y + d) % 8], ryb.at[d - 1], yb_send.at[d - 1], yb_recv.at[d - 1], y_peer[d]
        )
        last["yb", d].start()
    total = ya[y]
    for d in reversed(order):
        last["ya", d].wait_recv()
        total += rya[d - 1].astype(F32)
    ta[0:80] = total
    for n in range(8):
        sza[n] = ta[10 * n : 10 * n + 16].astype(BF16)
    for d in order:
        last["za", d] = remote(
            sza.at[(z + d) % 8], rza.at[d - 1], za_send.at[d - 1], za_recv.at[d - 1], z_peer[d]
        )
        last["za", d].start()
    total_b = tb[y]
    for d in reversed(order):
        last["yb", d].wait_recv()
        total_b += ryb[d - 1]
    total_a = sza[z].astype(F32)
    for d in reversed(order):
        last["za", d].wait_recv()
        total_a += rza[d - 1].astype(F32)
    fin[0:16] = total_a * (1.0 / 8.0)
    fin[10:18] = total_b * (1.0 / 8.0)
    out_ref[...] = fin[0:18, 0:96]

    started = list(wx.values()) + list(wc.values()) + list(halo.values()) + list(back.values())
    started += list(core.values()) + list(cross.values()) + list(last.values()) + [tokens_out]
    for copy in started:
        copy.wait_send()
    write_att.wait()
    write_gtok.wait()


def local(tokens, w_qkv, score_scale, grad_out):
    dma = pltpu.SemaphoreType.DMA
    vmem = pl.BlockSpec(memory_space=pltpu.VMEM)
    anywhere = pl.BlockSpec(memory_space=pl.ANY)
    shapes = (
        jax.ShapeDtypeStruct((256, 384), BF16),
        jax.ShapeDtypeStruct((256, 768), BF16),
        jax.ShapeDtypeStruct((18, 96), F32),
    )
    attended, grad_tokens, weight_grad = pl.pallas_call(
        kernel,
        out_shape=shapes,
        in_specs=[anywhere] * 4,
        out_specs=(anywhere, anywhere, vmem),
        scratch_shapes=[
            pltpu.VMEM((512, 768), BF16),
            pltpu.VMEM((256, 384), BF16),
            pltpu.SMEM((6,), F32),
            pltpu.VMEM((256, 384), BF16),
            pltpu.VMEM((256, 768), BF16),
            pltpu.VMEM((3, 768, 384), BF16),
            pltpu.VMEM((4, 2, 96, 256), BF16),
            pltpu.VMEM((4, 96, 512), BF16),
            pltpu.VMEM((512, 256), F32),
            pltpu.VMEM((256, 256), BF16),
            pltpu.VMEM((256, 256), BF16),
            pltpu.VMEM((3, 256, 256), BF16),
            pltpu.VMEM((3, 256, 256), F32),
            pltpu.VMEM((3, 2, 256, 128), BF16),
            pltpu.VMEM((3, 2, 256, 128), BF16),
            pltpu.VMEM((3, 512, 256), BF16),
            pltpu.VMEM((256, 768), BF16),
            pltpu.VMEM((3, 256, 256), F32),
            pltpu.VMEM((3, 256, 256), BF16),
            pltpu.VMEM((3, 256, 256), BF16),
            pltpu.VMEM((3, 512, 384), BF16),
            pltpu.VMEM((3, 3, 96, 384), BF16),
            pltpu.VMEM((3, 3, 96, 384), BF16),
            pltpu.VMEM((3, 128, 384), F32),
            pltpu.VMEM((1152, 128), F32),
            pltpu.VMEM((8, 80, 128), F32),
            pltpu.VMEM((8, 64, 128), F32),
            pltpu.VMEM((8, 80, 128), BF16),
            pltpu.VMEM((8, 64, 128), BF16),
            pltpu.VMEM((7, 80, 128), BF16),
            pltpu.VMEM((7, 64, 128), BF16),
            pltpu.VMEM((88, 128), F32),
            pltpu.VMEM((8, 8, 128), F32),
            pltpu.VMEM((8, 16, 128), BF16),
            pltpu.VMEM((7, 16, 128), BF16),
            pltpu.VMEM((7, 8, 128), F32),
            pltpu.VMEM((24, 128), F32),
            dma((3,)), dma((3, 3)), dma((2,)), dma((3, 3)), dma((3, 3)), dma((3, 4)), dma((3, 4)),
            dma((8,)), dma((8,)), dma((3, 8)), dma((3, 8)),
            dma, dma, dma((3, 2)), dma((3, 2)), dma((3, 2, 3)), dma((3, 2, 3)),
            dma((7,)), dma((7,)), dma((2, 7)), dma((2, 7)), dma((7,)), dma((7,)), dma((7,)), dma((7,)),
        ],
        compiler_params=pltpu.CompilerParams(
            collective_id=0, has_side_effects=True, vmem_limit_bytes=63 * 1024 * 1024
        ),
    )(tokens.reshape(256, 768), w_qkv, score_scale, grad_out.reshape(256, 384))
    return (
        attended.reshape(1, 1, 16, 16, 384),
        grad_tokens.reshape(1, 1, 16, 16, 768),
        weight_grad.T,
    )


def solution(mesh):
    return jax.shard_map(
        local,
        mesh=mesh,
        in_specs=(
            P("img", "sp", None, None, None),
            P("img", None),
            P(),
            P("img", "sp", None, None, None),
        ),
        out_specs=(
            P("img", "sp", None, None, None),
            P("img", "sp", None, None, None),
            P("img", "sp"),
        ),
        check_vma=False,
    )
```

```python
import jax
import jax.numpy as jnp
from jax import lax
from jax.experimental import pallas as pl
from jax.experimental.pallas import tpu as pltpu
from jax.sharding import PartitionSpec as P

MESH = pl.DeviceIdType.MESH
BF16 = jnp.bfloat16
F32 = jnp.float32
NORM_EPS = 1e-06
NEVER = -1e30
STRIPS = (
    (-1, 0, 0, 48),
    (1, 0, 48, 48),
    (0, -1, 96, 48),
    (0, 1, 144, 48),
    (-1, -1, 192, 16),
    (-1, 1, 208, 16),
    (1, -1, 224, 16),
    (1, 1, 240, 16),
)


def remote(src, dst, send, recv, device):
    return pltpu.make_async_remote_copy(
        src_ref=src,
        dst_ref=dst,
        send_sem=send,
        recv_sem=recv,
        device_id=device,
        device_id_type=MESH,
    )


def dot(a, b):
    return jnp.dot(a, b, preferred_element_type=F32)


def dot_nt(a, b):
    return lax.dot_general(a, b, (((1,), (1,)), ((), ())), preferred_element_type=F32)


def halo_place(j):
    strip = (j >= 48).astype(jnp.int32) + (j >= 96).astype(jnp.int32) + (j >= 144).astype(jnp.int32)
    m = j - 48 * strip
    edge = m >> 4
    along = m & 15
    low = jnp.where((strip & 1) == 0, -3, 16)
    step = jnp.where((strip & 1) == 0, -1, 1)
    level = strip < 2
    row_e = jnp.where(level, low + edge, along)
    col_e = jnp.where(level, along, low + edge)
    rstep_e = jnp.where(level, step, 0)
    cstep_e = jnp.where(level, 0, step)
    k = j - 192
    corner = k >> 4
    n = k & 15
    r3 = n >> 2
    c3 = n & 3
    rstep_c = jnp.where((corner & 2) == 0, -1, 1)
    cstep_c = jnp.where((corner & 1) == 0, -1, 1)
    row_c = jnp.where(rstep_c < 0, -3, 16) + r3
    col_c = jnp.where(cstep_c < 0, -3, 16) + c3
    is_edge = j < 192
    row = jnp.where(is_edge, row_e, row_c)
    col = jnp.where(is_edge, col_e, col_c)
    rstep = jnp.where(is_edge, rstep_e, rstep_c)
    cstep = jnp.where(is_edge, cstep_e, cstep_c)
    filled = is_edge | ((r3 < 3) & (c3 < 3))
    return row, col, rstep, cstep, filled


def owner_token(j):
    row, col, rstep, cstep, filled = halo_place(j)
    return jnp.where(filled, (row - 16 * rstep) * 16 + (col - 16 * cstep), -1)


def kernel(
    tok_hbm, w_hbm, scale_hbm, g_hbm, att_hbm, gtok_hbm, out_ref,
    tokx, g_ref, scale_ref, att_ref, gtok_ref, wp, tok_t, tok_2, bias, pack, unpack, qk, inv, qum, gm, kvx, hs, own,
    ghs, ghr, gq, s2, r2, acc, acc_t, ya, zb, sya, szb, rya, rzb, ta, tb, sza, rza, ryb, fin,
    in_sem, w_sem, out_sem, wx_send, wx_recv, wc_send, wc_recv, h_send, h_recv, gh_send, gh_recv,
    tok_send, tok_recv, core_send, core_recv, x_send, x_recv, ya_send, ya_recv, zb_send, zb_recv,
    za_send, za_recv, yb_send, yb_recv,
):
    img = lax.axis_index("img")
    sp = lax.axis_index("sp")
    x, c = img // 2, img % 2
    y, z = sp // 8, sp % 8
    other_core = (2 * x + 1 - c, sp)
    x_peer = [((2 * ((x + d) % 4) + c), sp) for d in range(4)]
    y_peer = [(img, 8 * ((y + d) % 8) + z) for d in range(8)]
    z_peer = [(img, 8 * y + (z + d) % 8) for d in range(8)]

    def tile_at(rstep, cstep):
        return (img, 8 * ((y + rstep + 8) % 8) + (z + cstep + 8) % 8)

    def block(b):
        return pl.ds(pl.multiple_of(96 * b, 32), 96)

    loads = [
        pltpu.make_async_copy(tok_hbm, tokx.at[pl.ds(0, 256)], in_sem.at[0]),
        pltpu.make_async_copy(g_hbm, g_ref, in_sem.at[1]),
        pltpu.make_async_copy(scale_hbm, scale_ref, in_sem.at[2]),
    ]
    w_loads = [
        pltpu.make_async_copy(
            w_hbm.at[:, pl.ds(384 * part + 128 * p, 128)],
            wp.at[p, block(img), pl.ds(128 * part, 128)],
            w_sem.at[p, part],
        )
        for p in range(3)
        for part in range(3)
    ]
    barrier = pltpu.get_barrier_semaphore()
    peers = [other_core] + x_peer[1:] + y_peer[1:] + z_peer[1:]
    peers += [tile_at(r, s) for r in (-1, 1) for s in (-1, 1)]
    for peer in peers[:4]:
        pl.semaphore_signal(barrier, inc=1, device_id=peer, device_id_type=MESH)
    for load in w_loads + loads[:1]:
        load.start()
    for peer in peers[4:]:
        pl.semaphore_signal(barrier, inc=1, device_id=peer, device_id_type=MESH)
    for load in loads[1:]:
        load.start()

    j_rows = lax.broadcasted_iota(jnp.int32, (256, 1), 0)
    j_cols = lax.broadcasted_iota(jnp.int32, (1, 256), 1)
    wide_rows = lax.broadcasted_iota(jnp.int32, (256, 256), 0)
    wide_cols = lax.broadcasted_iota(jnp.int32, (256, 256), 1)
    pack[...] = jnp.where(owner_token(j_rows) == wide_cols, 1.0, 0.0).astype(BF16)

    for load in w_loads:
        load.wait()
    pl.semaphore_wait(barrier, len(peers))

    wx, wc = {}, {}

    def to_core(p, n, ref):
        wc[p, n] = remote(ref, ref, wc_send.at[p, n], wc_recv.at[p, n], other_core)
        wc[p, n].start()

    def to_x(p, n, ref, d):
        wx[p, n] = remote(ref, ref, wx_send.at[p, n], wx_recv.at[p, n], x_peer[d])
        wx[p, n].start()

    def half(b, h):
        return pl.ds(pl.multiple_of(96 * b + 48 * h, 16), 48)

    left, right, across = [2 * ((x + d) % 4) + c for d in (3, 1, 2)]

    def share(p):
        mine = wp.at[p, block(img)]
        to_x(p, 2, mine, 2)
        to_x(p, 0, mine, 1)
        to_x(p, 1, mine, 3)
        to_core(p, 0, mine)

    def pass_on(p):
        wx[p, 0].wait_recv()
        to_core(p, 1, wp.at[p, block(left)])
        wx[p, 1].wait_recv()
        to_core(p, 2, wp.at[p, block(right)])

    def pass_core(p):
        wx[p, 2].wait_recv()
        to_core(p, 3, wp.at[p, block(across)])

    for p in range(3):
        share(p)

    for load in loads:
        load.wait()
    hs[...] = dot(pack[...], tokx[0:256]).astype(BF16)
    halo = {}
    for s, (rstep, cstep, first, rows) in reversed(list(enumerate(STRIPS))):
        halo[s] = remote(
            hs.at[pl.ds(first, rows)],
            tokx.at[pl.ds(256 + first, rows)],
            h_send.at[s],
            h_recv.at[s],
            tile_at(-rstep, -cstep),
        )
        halo[s].start()

    query = lax.broadcasted_iota(jnp.int32, (1, 256), 1)
    query_row, query_col = query >> 4, query & 15

    def put_bias(low, key_row, key_col):
        near = (jnp.abs(key_row - query_row) <= 3) & (jnp.abs(key_col - query_col) <= 3)
        bias[low : low + 256] = jnp.where(near, 0.0, NEVER).astype(F32)

    put_bias(0, j_rows >> 4, j_rows & 15)
    row, col, _, _, filled = halo_place(j_rows)
    grow, gcol = row + 16 * y, col + 16 * z
    inside = filled & (grow >= 0) & (grow < 128) & (gcol >= 0) & (gcol < 128)
    put_bias(256, jnp.where(inside, row, 1000), col)
    unpack[...] = jnp.where(owner_token(j_cols) == wide_rows, 1.0, 0.0).astype(BF16)
    lane_r = lax.broadcasted_iota(jnp.int32, (128, 128), 0)
    lane_c = lax.broadcasted_iota(jnp.int32, (128, 128), 1)
    same_head = jnp.where((lane_r >> 6) == (lane_c >> 6), 1.0, 0.0).astype(BF16)
    eye = jnp.where(lane_r == lane_c, 1.0, 0.0).astype(BF16)
    lane = lax.broadcasted_iota(jnp.int32, (1, 128), 1)
    head_mask = [jnp.where((lane >> 6) == e, 1.0, 0.0).astype(F32) for e in range(2)]

    for p in range(3):
        g_pair = g_ref[:, 128 * p : 128 * p + 128].astype(F32)
        for e in range(2):
            gm[p, e] = (g_pair * head_mask[e]).astype(BF16)

    for b in range(8):
        tok_t[b // 2, b % 2] = tokx[0:256, 96 * b : 96 * b + 96].astype(F32).T.astype(BF16)
    tokens_out = remote(
        tok_t.at[:, 1 - c], tok_2.at[:, :, pl.ds(256, 256)], tok_send, tok_recv, other_core
    )
    tokens_out.start()
    tok_2[:, :, 0:256] = tok_t[:, c]
    acc[:, 96:128, :] = jnp.zeros((3, 32, 384), F32)
    ta[80:88] = jnp.zeros((8, 128), F32)

    def head_sum(v):
        high = v.astype(BF16)
        low = (v - high.astype(F32)).astype(BF16)
        return dot(high, same_head) + dot(low, same_head)

    back, core, cross = {}, {}, {}

    def exchange(p, n, lanes):
        core[p, n] = remote(
            gq.at[p, pl.ds(0, 256), lanes],
            gq.at[p, pl.ds(256, 256), lanes],
            core_send.at[p, n],
            core_recv.at[p, n],
            other_core,
        )
        core[p, n].start()

    def project(p):
        for d in range(4):
            wc[p, d].wait_recv()
        low = dot(tokx[0:256], wp[p]).astype(BF16)
        far = dot(tokx[256:512], wp[p, :, 128:384]).astype(BF16)
        qk[p] = low[:, 0:256]
        q = low[:, 0:128].astype(F32)
        k = low[:, 128:256].astype(F32)
        k_far = far[:, 0:128].astype(F32)
        inv_q = lax.rsqrt(head_sum(q * q) * (1.0 / 64.0) + NORM_EPS) * 0.125
        inv_k = lax.rsqrt(head_sum(k * k) * (1.0 / 64.0) + NORM_EPS) * 0.125
        inv_far = lax.rsqrt(head_sum(k_far * k_far) * (1.0 / 64.0) + NORM_EPS) * 0.125
        inv[p, :, 0:128] = inv_q
        inv[p, :, 128:256] = inv_k
        q_unit = q * inv_q
        for e in range(2):
            qum[p, e] = (q_unit * head_mask[e]).astype(BF16)
        kvx[p, 0:256, 0:128] = (k * inv_k).astype(BF16)
        kvx[p, 0:256, 128:256] = low[:, 256:384]
        kvx[p, 256:512, 0:128] = (k_far * inv_far).astype(BF16)
        kvx[p, 256:512, 128:256] = far[:, 128:256]

    def attend(p):
        key = kvx[p, :, 0:128]
        value = kvx[p, :, 128:256]
        lows, grads = [], []
        for e in range(2):
            scale = scale_ref[2 * p + e]
            raised = jnp.exp(dot_nt(key, qum[p, e]) * scale + bias[...])
            attention = raised * (1.0 / jnp.sum(raised, axis=0, keepdims=True))
            grad_att = dot_nt(value, gm[p, e])
            row_total = jnp.sum(attention * grad_att, axis=0, keepdims=True)
            lows.append(attention.astype(BF16))
            grads.append((attention * scale * (grad_att - row_total)).astype(BF16))

        def key_side(first):
            rows = slice(first, first + 256)
            grad_k = dot(grads[0][rows], qum[p, 0]) + dot(grads[1][rows], qum[p, 1])
            grad_v = dot(lows[0][rows], gm[p, 0]) + dot(lows[1][rows], gm[p, 1])
            return grad_k, grad_v

        grad_k, grad_v = key_side(256)
        ghs[p, :, 0:128] = grad_k.astype(BF16)
        ghs[p, :, 128:256] = grad_v.astype(BF16)
        for s, (rstep, cstep, first, rows) in reversed(list(enumerate(STRIPS))):
            span = pl.ds(first, rows)
            back[p, s] = remote(
                ghs.at[p, span], ghr.at[p, span], gh_send.at[p, s], gh_recv.at[p, s], tile_at(rstep, cstep)
            )
            back[p, s].start()
        key_t = dot_nt(eye, key).astype(BF16)
        value_t = dot_nt(eye, value).astype(BF16)
        att_t, gq_t = [], []
        for e in range(2):
            rows = slice(64 * e, 64 * e + 64)
            gq_t.append(dot(key_t[rows], grads[e]))
            att_t.append(dot(value_t[rows], lows[e]))
        grad_q = jnp.concatenate(gq_t, axis=0).T
        q = qk[p, :, 0:128].astype(F32)
        inv_q = inv[p, :, 0:128]
        gq[p, 0:256, 0:128] = (inv_q * (grad_q - q * (inv_q * inv_q) * head_sum(grad_q * q))).astype(BF16)
        exchange(p, 0, pl.ds(0, 128))
        grad_k, grad_v = key_side(0)
        own[p, :, 0:128] = grad_k
        own[p, :, 128:256] = grad_v
        att_ref[:, 128 * p : 128 * p + 128] = jnp.concatenate(att_t, axis=0).T.astype(BF16)

    def finish(p):
        for s in range(8):
            back[p, s].wait_recv()
        grad_kv = own[p] + dot(unpack[...], ghr[p])
        grad_k = grad_kv[:, 0:128]
        k = qk[p, :, 128:256].astype(F32)
        inv_k = inv[p, :, 128:256]
        gq[p, 0:256, 128:256] = (inv_k * (grad_k - k * (inv_k * inv_k) * head_sum(grad_k * k))).astype(BF16)
        gq[p, 0:256, 256:384] = grad_kv[:, 128:256].astype(BF16)
        exchange(p, 1, pl.ds(128, 256))

    def cross_send(p, part):
        core[p, part].wait_recv()
        lanes = slice(128, 384) if part else slice(0, 128)
        span = pl.ds(128, 256) if part else pl.ds(0, 128)
        mine = gq[p, :, lanes]
        for d in (2, 1, 3):
            s2[p, d - 1, :, lanes] = dot(tok_2[(x + d) % 4], mine).astype(BF16)
            cross[p, part, d] = remote(
                s2.at[p, d - 1, :, span],
                r2.at[p, d - 1, :, span],
                x_send.at[p, part, d - 1],
                x_recv.at[p, part, d - 1],
                x_peer[d],
            )
            cross[p, part, d].start()
        acc[p, 0:96, lanes] = dot(tok_2[x], mine)

    stages = [(0, 0), (1, 0), (0, 1), (2, 0), (1, 1), (2, 1)]

    def stage_of(n):
        return stages.index((n % 384 // 128, min(n // 384, 1)))

    def cross_sum(p, part):
        lanes = slice(128, 384) if part else slice(0, 128)
        for d in (1, 3, 2):
            cross[p, part, d].wait_recv()
        total = acc[p, 0:96, lanes]
        for d in range(3):
            total += r2[p, d, :, lanes].astype(F32)
        acc[p, 0:96, lanes] = total
        for n in (1, 2) if part else (0,):
            low = 384 * n + 128 * p
            acc_t[low : low + 128] = acc[p, :, 128 * n : 128 * n + 128].T
        for s in range(64):
            if max(stage_of(18 * s + i) for i in range(18)) == stages.index((p, part)):
                ya[s // 8, 10 * (s % 8) : 10 * (s % 8) + 10] = acc_t[18 * s : 18 * s + 10]
                zb[s % 8, 8 * (s // 8) : 8 * (s // 8) + 8] = acc_t[18 * s + 10 : 18 * s + 18]

    pass_on(0)
    pass_core(0)
    for s in range(8):
        halo[s].wait_recv()
    project(0)
    attend(0)
    pass_on(1)
    pass_core(1)
    project(1)
    tokens_out.wait_recv()
    cross_send(0, 0)
    attend(1)
    pass_on(2)
    pass_core(2)
    finish(0)
    cross_send(1, 0)
    project(2)
    attend(2)
    write_att = pltpu.make_async_copy(att_ref, att_hbm, out_sem.at[0])
    write_att.start()
    cross_send(0, 1)
    finish(1)
    cross_send(2, 0)
    cross_send(1, 1)
    finish(2)
    cross_sum(0, 0)
    cross_sum(1, 0)
    cross_send(2, 1)
    grad_tokens = dot_nt(gq[0, 0:256], wp[0]) + dot_nt(gq[1, 0:256], wp[1]) + dot_nt(gq[2, 0:256], wp[2])
    gtok_ref[...] = grad_tokens.astype(BF16)
    write_gtok = pltpu.make_async_copy(gtok_ref, gtok_hbm, out_sem.at[1])
    write_gtok.start()
    cross_sum(0, 1)
    cross_sum(2, 0)
    cross_sum(1, 1)

    last = {}
    order = (4, 3, 5, 2, 6, 1, 7)
    for d in order:
        last["ya", d] = remote(
            sya.at[(y + d) % 8], rya.at[d - 1], ya_send.at[d - 1], ya_recv.at[d - 1], y_peer[d]
        )
        for h in range(2):
            rows = pl.ds(32 * h, 32)
            last["zb", h, d] = remote(
                szb.at[(z + d) % 8, rows], rzb.at[d - 1, rows], zb_send.at[h, d - 1], zb_recv.at[h, d - 1], z_peer[d]
            )

    def waits_for_last(row):
        return (row == 4) | (row == 5) | (row == 7)

    sya[0:4] = ya[0:4].astype(BF16)
    sya[6] = ya[6].astype(BF16)
    szb[:, 0:32] = zb[:, 0:32].astype(BF16)
    for d in order:
        pl.when(jnp.logical_not(waits_for_last((y + d) % 8)))(last["ya", d].start)
        last["zb", 0, d].start()
    cross_sum(2, 1)

    sya[4:6] = ya[4:6].astype(BF16)
    sya[7] = ya[7].astype(BF16)
    szb[:, 32:64] = zb[:, 32:64].astype(BF16)
    for d in order:
        pl.when(waits_for_last((y + d) % 8))(last["ya", d].start)
        last["zb", 1, d].start()
    total = zb[z]
    for d in reversed(order):
        last["zb", 0, d].wait_recv()
        last["zb", 1, d].wait_recv()
        total += rzb[d - 1].astype(F32)
    for n in range(8):
        tb[n] = total[8 * n : 8 * n + 8]
    for d in order:
        last["yb", d] = remote(
            tb.at[(y + d) % 8], ryb.at[d - 1], yb_send.at[d - 1], yb_recv.at[d - 1], y_peer[d]
        )
        last["yb", d].start()
    total = ya[y]
    for d in reversed(order):
        last["ya", d].wait_recv()
        total += rya[d - 1].astype(F32)
    ta[0:80] = total
    for n in range(8):
        sza[n] = ta[10 * n : 10 * n + 16].astype(BF16)
    for d in order:
        last["za", d] = remote(
            sza.at[(z + d) % 8], rza.at[d - 1], za_send.at[d - 1], za_recv.at[d - 1], z_peer[d]
        )
        last["za", d].start()
    total_b = tb[y]
    for d in reversed(order):
        last["yb", d].wait_recv()
        total_b += ryb[d - 1]
    total_a = sza[z].astype(F32)
    for d in reversed(order):
        last["za", d].wait_recv()
        total_a += rza[d - 1].astype(F32)
    fin[0:16] = total_a * (1.0 / 8.0)
    fin[10:18] = total_b * (1.0 / 8.0)
    out_ref[...] = fin[0:18, 0:96]

    started = list(wx.values()) + list(wc.values()) + list(halo.values()) + list(back.values())
    started += list(core.values()) + list(cross.values()) + list(last.values()) + [tokens_out]
    for copy in started:
        copy.wait_send()
    write_att.wait()
    write_gtok.wait()


def local(tokens, w_qkv, score_scale, grad_out):
    dma = pltpu.SemaphoreType.DMA
    vmem = pl.BlockSpec(memory_space=pltpu.VMEM)
    anywhere = pl.BlockSpec(memory_space=pl.ANY)
    shapes = (
        jax.ShapeDtypeStruct((256, 384), BF16),
        jax.ShapeDtypeStruct((256, 768), BF16),
        jax.ShapeDtypeStruct((18, 96), F32),
    )
    attended, grad_tokens, weight_grad = pl.pallas_call(
        kernel,
        out_shape=shapes,
        in_specs=[anywhere] * 4,
        out_specs=(anywhere, anywhere, vmem),
        scratch_shapes=[
            pltpu.VMEM((512, 768), BF16),
            pltpu.VMEM((256, 384), BF16),
            pltpu.SMEM((6,), F32),
            pltpu.VMEM((256, 384), BF16),
            pltpu.VMEM((256, 768), BF16),
            pltpu.VMEM((3, 768, 384), BF16),
            pltpu.VMEM((4, 2, 96, 256), BF16),
            pltpu.VMEM((4, 96, 512), BF16),
            pltpu.VMEM((512, 256), F32),
            pltpu.VMEM((256, 256), BF16),
            pltpu.VMEM((256, 256), BF16),
            pltpu.VMEM((3, 256, 256), BF16),
            pltpu.VMEM((3, 256, 256), F32),
            pltpu.VMEM((3, 2, 256, 128), BF16),
            pltpu.VMEM((3, 2, 256, 128), BF16),
            pltpu.VMEM((3, 512, 256), BF16),
            pltpu.VMEM((256, 768), BF16),
            pltpu.VMEM((3, 256, 256), F32),
            pltpu.VMEM((3, 256, 256), BF16),
            pltpu.VMEM((3, 256, 256), BF16),
            pltpu.VMEM((3, 512, 384), BF16),
            pltpu.VMEM((3, 3, 96, 384), BF16),
            pltpu.VMEM((3, 3, 96, 384), BF16),
            pltpu.VMEM((3, 128, 384), F32),
            pltpu.VMEM((1152, 128), F32),
            pltpu.VMEM((8, 80, 128), F32),
            pltpu.VMEM((8, 64, 128), F32),
            pltpu.VMEM((8, 80, 128), BF16),
            pltpu.VMEM((8, 64, 128), BF16),
            pltpu.VMEM((7, 80, 128), BF16),
            pltpu.VMEM((7, 64, 128), BF16),
            pltpu.VMEM((88, 128), F32),
            pltpu.VMEM((8, 8, 128), F32),
            pltpu.VMEM((8, 16, 128), BF16),
            pltpu.VMEM((7, 16, 128), BF16),
            pltpu.VMEM((7, 8, 128), F32),
            pltpu.VMEM((24, 128), F32),
            dma((3,)), dma((3, 3)), dma((2,)), dma((3, 3)), dma((3, 3)), dma((3, 4)), dma((3, 4)),
            dma((8,)), dma((8,)), dma((3, 8)), dma((3, 8)),
            dma, dma, dma((3, 2)), dma((3, 2)), dma((3, 2, 3)), dma((3, 2, 3)),
            dma((7,)), dma((7,)), dma((2, 7)), dma((2, 7)), dma((7,)), dma((7,)), dma((7,)), dma((7,)),
        ],
        compiler_params=pltpu.CompilerParams(
            collective_id=0, has_side_effects=True, vmem_limit_bytes=63 * 1024 * 1024
        ),
    )(tokens.reshape(256, 768), w_qkv, score_scale, grad_out.reshape(256, 384))
    return (
        attended.reshape(1, 1, 16, 16, 384),
        grad_tokens.reshape(1, 1, 16, 16, 768),
        weight_grad.T,
    )


def solution(mesh):
    return jax.shard_map(
        local,
        mesh=mesh,
        in_specs=(
            P("img", "sp", None, None, None),
            P("img", None),
            P(),
            P("img", "sp", None, None, None),
        ),
        out_specs=(
            P("img", "sp", None, None, None),
            P("img", "sp", None, None, None),
            P("img", "sp"),
        ),
        check_vma=False,
    )
```
